128 devices in a mesh: grp: 4 (over x_hi, core), rel: 32 (over x_lo, y, z).
Axes of the slice: x: 4 (x_hi: 2, x_lo: 2; x = x_hi * 2 + x_lo), y: 4, z: 4, core: 2. Of those that a mesh axis runs over, the one named last changes fastest.
Arguments:
- head_ids: int32 [262144], P(('grp', 'rel')), may hold values from 0 to 1023
- relations: int32 [262144, 1], P(('grp', 'rel')), may hold values from 0 to 127; in each aligned block of 2048 rows (0 to 2047, 2048 to 4095, ...) at most 32 rows name the same one
- tail_ids: int32 [262144], P(('grp', 'rel')), may hold values from 0 to 1023
- neg_owner: int32 [1], replicated, may hold values from 0 to 127
- entities: bfloat16 [131072, 512], P(('grp', 'rel')), may hold values from -0.3984375 to 0.3984375
- rel_weight: float32 [128, 512, 512], P('rel'), may hold values from -6 to 6
- rel_accum: float32 [128, 512], P('rel'), may hold values from 0.001 to 0.1
Outputs:
- losses: bfloat16 [262144], P(('grp', 'rel'))
- head_grad: bfloat16 [262144, 512], P(('grp', 'rel'))
- new_rel: float32 [128, 512, 512], P('rel')
- new_accum: float32 [128, 512], P('rel')
The draws below stay inside these ranges and needn't reach their ends.
Inputs may be any that keep to these rules, and one draw needn't show every extreme that they name: `head_ids`: a row of the device's own shard of 1024 entity rows. `tail_ids`: a row of the device's own shard of 1024 entity rows. `relations`: in the 2048 rows of one device no relation is named by more than 32 rows; some relation is named by exactly 32. `neg_owner`: a device index, counted grp first, then rel.
All inputs are finite; a program needn't handle non-finite values.
Results may differ from the reference program's by a relative error of at most 0.0095.
Values may be sent and summed in bfloat16 or wider, within the bound.
A program may use at most 128 MiB of HBM per device.

```python
import math
import jax
import jax.numpy as jnp
import numpy as np
from jax import lax

D = 512
NEG = 1024
TRIP_DEV = 2048
GROUPS = 4
OWNERS = 32
RELS = 128
CAPR = 32
TRIPLES = 262144
ENTS = 131072
DEVICES = 128


def with_ends(result, stream_key, least, high):
    extent = result.shape
    place = [jax.random.randint(jax.random.fold_in(stream_key, axis), (), 0, extent[axis]) for axis in range(len(extent))]
    result = result.at[tuple(place)].set(least)
    longest = extent.index(max(extent))
    place[longest] = (place[longest] + 1) % extent[longest]
    return result.at[tuple(place)].set(high)


def level_of(key, dims, shards, smallest, high):
    factor_of, own = 1.0, jax.random.fold_in(key, 6)
    for axis_at, shards_of in shards:
        draws = jnp.exp(jax.random.uniform(jax.random.fold_in(own, axis_at), (shards_of,), jnp.float32, smallest / len(shards), high / len(shards)))
        factor_of = factor_of * jnp.repeat(draws, dims[axis_at] // shards_of).reshape([-1 if axis == axis_at else 1 for axis in range(len(dims))])
    return factor_of


def assign_block(key, own, number, rows, number_of, top, limit, slope):
    order = jax.random.permutation(key, number_of)
    crowded, usual = portions_of(number_of, rows * top, limit, slope, True), portions_of(number_of, rows * top, limit, slope, False)
    places = jnp.arange(number_of)

    def named(lengths, offset_by):
        used = int((lengths > 0).sum())
        fixed = max(1, used // 4)
        shifted = fixed + (places - fixed + offset_by * (used - fixed)) % max(1, number_of - fixed)
        return jnp.zeros((number_of,), jnp.int32).at[order[jnp.where(places < fixed, places, shifted)]].set(jnp.asarray(lengths, jnp.int32))

    lengths = jnp.where(number % 4 == 0, named(crowded, number // 4), named(usual, number - number // 4 - 1))
    mixed = jax.random.permutation(jax.random.fold_in(own, 3), number_of)
    donor, taker = mixed[0:number_of // 2 * 2:2], mixed[1:number_of // 2 * 2:2]
    margin = jnp.minimum(lengths[donor] - 1, limit - lengths[taker]) // 2
    margin = jnp.where((donor == order[0]) | (taker == order[0]) | (lengths[taker] == 0), 0, jnp.maximum(margin, 0))
    shifted = jax.random.randint(jax.random.fold_in(own, 4), (number_of // 2,), 0, 1 << 20) % (margin + 1)
    lengths = lengths.at[donor].add(-shifted).at[taker].add(shifted)
    labels = jnp.searchsorted(jnp.cumsum(lengths), jnp.arange(rows * top), side="right").astype(jnp.int32)
    table = labels.reshape(top, rows).T
    table = table[jax.random.permutation(jax.random.fold_in(own, 1), rows)]
    offset_by = jax.random.randint(jax.random.fold_in(own, 2), (rows, 1), 0, top)
    return jnp.take_along_axis(table, (jnp.arange(top)[None, :] + offset_by) % top, axis=1)


def portions_of(count, total, most, skew, full):
    portions = [(1 << 20) // math.isqrt(grade ** skew) + 1 for grade in range(1, count + 1)]
    largest = most if full else min(most, max(-(-total // count), total * portions[0] // sum(portions)))
    least = 1 if total - largest >= count - 1 else 0
    counts, rest = [largest] + [least] * (count - 1), total - largest - least * (count - 1)
    while rest > 0:
        free = [i for i in range(1, count) if counts[i] < largest] or [i for i in range(1, count) if counts[i] < most]
        mass, remaining = sum([portions[i] for i in free]), rest
        for i in free:
            addition = min(most - counts[i], max(1, remaining * portions[i] // mass), rest)
            counts[i] = counts[i] + addition
            rest = rest - addition
    return np.array(counts)


def noise(stream_key, extent, deviation, bound, split=(), held_as=jnp.bfloat16):
    entries = jax.random.normal(stream_key, extent, jnp.float32) * deviation
    if len(split) > 0:
        entries = level_of(stream_key, extent, split, -0.22, 0.18) * entries
    return jnp.clip(entries, min=-bound, max=bound).astype(held_as)


def setup_inputs(seed: int = 0) -> dict:
    key_list = jax.random.split(jax.random.key(seed), 8)
    head_ids = with_ends(jax.random.randint(key_list[0], (TRIPLES,), 0, NEG), jax.random.fold_in(key_list[0], 1), 0, NEG - 1).astype(jnp.int32)
    relations_keys = jax.random.split(jax.random.fold_in(key_list[1], 1), TRIPLES // TRIP_DEV)
    relations_turns = jax.random.permutation(jax.random.fold_in(key_list[1], 3), TRIPLES // TRIP_DEV)
    relations = jax.vmap(lambda own, number: assign_block(jax.random.fold_in(key_list[1], 2), own, number, TRIP_DEV, RELS, 1, CAPR, 2))(relations_keys, relations_turns).reshape((TRIPLES, 1))
    tail_ids = with_ends(jax.random.randint(key_list[2], (TRIPLES,), 0, NEG), jax.random.fold_in(key_list[2], 1), 0, NEG - 1).astype(jnp.int32)
    neg_owner = jax.random.randint(key_list[3], (1,), 0, DEVICES).astype(jnp.int32)
    entities = noise(key_list[4], (ENTS, D), 0.1, 0.3984375, ((0, 128),))
    rel_weight = noise(key_list[5], (RELS, D, D), 1.0, 6.0, ((0, 32),), jnp.float32)
    rel_accum = jnp.clip(jnp.exp(math.log(0.1) - 4.6051702 * jax.random.uniform(key_list[6], (RELS, D), jnp.float32) ** level_of(key_list[6], (RELS, D), ((0, 32),), -0.2, 0.2)), 0.001, 0.1)
    return dict(head_ids=head_ids, relations=relations, tail_ids=tail_ids, neg_owner=neg_owner, entities=entities, rel_weight=rel_weight, rel_accum=rel_accum)


LEARNING_RATE = 1.0

def slot_ranks(rel_ids, bucket_count):
    one_hot = (rel_ids[..., None] == jnp.arange(bucket_count, dtype=jnp.int32)).astype(jnp.int32)
    running = jnp.cumsum(one_hot, axis=-2) - 1
    return lax.optimization_barrier(jnp.sum(one_hot * running, axis=-1)).astype(jnp.int32)

def score_rows(query_rows, tail_rows, negatives):
    positive = lax.optimization_barrier(jnp.sum(query_rows.astype(jnp.float32) * tail_rows.astype(jnp.float32), axis=-1))
    neg_scores = jnp.dot(query_rows, negatives.T, preferred_element_type=jnp.float32)
    losses = jax.nn.softplus(-positive) + lax.optimization_barrier(jnp.mean(jax.nn.softplus(neg_scores), axis=-1))
    coefs = (jax.nn.sigmoid(neg_scores) / negatives.shape[0]).astype(jnp.bfloat16)
    grad_query = -jax.nn.sigmoid(-positive)[:, None] * tail_rows.astype(jnp.float32)
    grad_query = grad_query + jnp.dot(coefs, negatives, preferred_element_type=jnp.float32)
    return (losses.astype(jnp.bfloat16), grad_query.astype(jnp.bfloat16))

def adagrad(weight, accumulator, gradient):
    new_accum = accumulator + lax.optimization_barrier(jnp.mean(gradient * gradient, axis=-1))
    return (weight - LEARNING_RATE * gradient / jnp.sqrt(new_accum)[..., None], new_accum)

def reference(head_ids, relations, tail_ids, neg_owner, entities, rel_weight, rel_accum):
    width = entities.shape[1]
    rel_ids = relations[:, 0].astype(jnp.int32)
    device = jnp.arange(TRIPLES, dtype=jnp.int32) // TRIP_DEV
    head_rows = jnp.take(entities, device * NEG + head_ids, axis=0)
    tail_rows = jnp.take(entities, device * NEG + tail_ids, axis=0)
    negatives = lax.dynamic_slice_in_dim(entities, (neg_owner[0] * NEG).astype(jnp.int32), NEG, 0)
    ranking = slot_ranks(rel_ids.reshape(DEVICES, TRIP_DEV), RELS).reshape(TRIPLES)
    flat_index = device * (RELS * CAPR) + rel_ids * CAPR + ranking
    matrices = rel_weight.astype(jnp.bfloat16)

    def by_relation(values):
        filled = jnp.zeros((DEVICES * RELS * CAPR, width), values.dtype).at[flat_index].set(values)
        return filled.reshape(DEVICES, RELS, CAPR, width).transpose(1, 0, 2, 3).reshape(RELS, DEVICES * CAPR, width)

    def by_triple(stacked):
        whole = stacked.reshape(RELS, DEVICES, CAPR, width).transpose(1, 0, 2, 3)
        return whole.reshape(DEVICES * RELS * CAPR, width)[flat_index]
    held_rows = by_relation(head_rows)

    def project(operands):
        rows_in, matrix = operands
        return jnp.dot(rows_in, matrix, preferred_element_type=jnp.float32).astype(jnp.bfloat16)
    projected = by_triple(lax.map(project, (held_rows, matrices)))

    def score_block(operands):
        query_block, tail_block = operands
        return score_rows(query_block, tail_block, negatives)
    losses, grad_query = lax.map(score_block, (projected.reshape(DEVICES, TRIP_DEV, width), tail_rows.reshape(DEVICES, TRIP_DEV, width)))
    grad_rows = by_relation(grad_query.reshape(TRIPLES, width))

    def backward(operands):
        rows_in, grad_in, matrix = operands
        head_back = jnp.dot(grad_in, matrix.T, preferred_element_type=jnp.float32).astype(jnp.bfloat16)
        rows_group = rows_in.reshape(GROUPS, OWNERS * CAPR, width).astype(jnp.float32)
        grad_group = grad_in.reshape(GROUPS, OWNERS * CAPR, width).astype(jnp.float32)
        partial_value = jnp.einsum('gnd,gne->gde', rows_group, grad_group).astype(jnp.bfloat16)
        partial_value = lax.optimization_barrier(partial_value)
        return (head_back, lax.optimization_barrier(jnp.sum(partial_value.astype(jnp.float32), axis=0)))
    head_stack, summed = lax.map(backward, (held_rows, grad_rows, matrices))
    head_grad = by_triple(head_stack)
    new_rel, new_accum = adagrad(rel_weight, rel_accum, summed)
    return (losses.reshape(TRIPLES), head_grad, new_rel, new_accum)
```

```python
import jax
import jax.numpy as jnp
from jax import lax
from jax.experimental import pallas as pl
from jax.experimental.pallas import tpu as pltpu
from jax.sharding import PartitionSpec as P

MESH = pl.DeviceIdType.MESH
BF, F32, I32 = jnp.bfloat16, jnp.float32, jnp.int32
ROWS, WIDTH, NEG = 2048, 512, 1024
CHUNKS, PEERS, CAP = 4, 32, 32
VMEM_BYTES = 58 * 2**20


def place():
    grp, rel = lax.axis_index("grp"), lax.axis_index("rel")
    x_hi, core = grp // 2, grp % 2
    x_lo, y, z = rel // 16, (rel // 4) % 4, rel % 4
    return x_hi, core, x_hi * 2 + x_lo, x_lo, y, z


def device_at(core, x, y, z):
    return ((x // 2) * 2 + core, (x % 2) * 16 + y * 4 + z)


def split_shift(n):
    b = (n * 5) % PEERS
    return b // 16, (b // 4) % 4, b % 4


def peer(n, sign, here):
    x_hi, core, x, x_lo, y, z = here
    dx, dy, dz = split_shift(n)
    x = (x + dx * (1 + 2 * (x % 2) + 2 * ((dy + dz) % 2))) % 4
    return device_at(core, x, (y + sign * dy + 4) % 4, (z + sign * dz + 4) % 4)


def prep_kernel(rel_ref, head_ref, tail_ref, table_ref, pos_ref):
    x_hi, core, x, x_lo, y, z = place()
    size = 256
    lane = lax.broadcasted_iota(I32, (size, 128), 1)
    lower = lax.broadcasted_iota(I32, (size, size), 0) > lax.broadcasted_iota(I32, (size, size), 1)
    lower = jnp.where(lower, 1.0, 0.0).astype(BF)

    def block(i, carry):
        seen, table = carry
        rows = pl.ds(pl.multiple_of(i * size, size), size)
        rel, head, tail = rel_ref[rows, :], head_ref[rows, :] + 1, tail_ref[rows, :] + 1
        hot = jnp.where(rel == lane, 1.0, 0.0)
        before = jnp.dot(lower, hot.astype(BF), preferred_element_type=F32) + seen
        rank = jnp.sum(hot * before, axis=1, keepdims=True).astype(I32)
        digit = jnp.where(lane < 64, jnp.where(lane < 32, head // 32, head % 32), jnp.where(lane < 96, tail // 32, tail % 32))
        marks = jnp.where(lane % 32 == rank, digit, 0).astype(F32).astype(BF)
        table = table + lax.dot_general(marks, hot.astype(BF), (((0,), (0,)), ((), ())), preferred_element_type=F32)
        owner = rel // 4
        b = ((owner // 16 + 2 - x_lo) % 2) * 16 + ((owner // 4 % 4 + 4 - y) % 4) * 4 + (owner % 4 + 4 - z) % 4
        pos_ref[rows, :] = (rel % 4) * (PEERS * CAP) + (b * 13 % PEERS) * CAP + rank
        return seen + jnp.sum(hot, axis=0, keepdims=True), table

    start = (jnp.zeros((1, 128), F32), jnp.zeros((128, 128), F32))
    _, table = lax.fori_loop(0, ROWS // size, block, start)
    table_ref[0:32, :] = table[0:32] * 32.0 + table[32:64] - 1.0
    table_ref[32:64, :] = table[64:96] * 32.0 + table[96:128] - 1.0


def main_kernel(
    owner_ref, ent_ref, table_ref, pos_ref, accum_ref, weight_ref,
    grad_ref, loss_ref, rel_ref, acc_ref,
    out_rows, in_rows, out_back, in_back, out_loss, in_loss, w32, w16, gbuf, lrow,
    own, g1s, g1r, g2s, g2r,
    neg, n0s, n0r, n1, n1r, n2, n2r, n3, n3r, n4,
    w_sem, rows_ss, rows_rs, back_ss, back_rs, loss_ss, loss_rs,
    neg_ss, neg_rs, grp_ss, grp_rs,
):
    here = place()
    x_hi, core, x, x_lo, y, z = here
    me = lax.axis_index("grp") * PEERS + lax.axis_index("rel")
    mate = device_at(1 - core, x, y, z)
    across = device_at(core, (x + 2) % 4, y, z)
    beside = device_at(core, (x + 3 + 2 * (x % 2)) % 4, y, z)
    quarter = core * 2 + x_hi

    def remote(src, dst, ss, rs, device):
        return pltpu.make_async_remote_copy(src_ref=src, dst_ref=dst, send_sem=ss, recv_sem=rs, device_id=device, device_id_type=MESH)

    w_copy = pltpu.make_async_copy(weight_ref, w32, w_sem)
    w_copy.start()

    barrier = pltpu.get_barrier_semaphore()

    def greet(n, c):
        pl.semaphore_signal(barrier, inc=1, device_id=peer(n, 1, here), device_id_type=MESH)
        return c

    lax.fori_loop(1, PEERS, greet, 0)
    for device in (mate, across, beside):
        pl.semaphore_signal(barrier, inc=1, device_id=device, device_id_type=MESH)
    pl.semaphore_wait(barrier, PEERS + 2)

    mine = (owner_ref[0] == me).astype(F32).astype(BF)

    def ring(axis, d):
        if axis == 0:
            return device_at(core, (x + d) % 4, y, z), (x + d) % 4
        if axis == 1:
            return device_at(core, x, (y + d) % 4, z), (y + d) % 4
        return device_at(core, x, y, (z + d) % 4), (z + d) % 4

    def rows_of(start, size):
        return pl.ds(pl.multiple_of(start, size), size)

    block32 = core * 512 + x * 128 + y * 32

    def neg_copies(stage):
        if stage == 0:
            return [remote(n0s, n0r, neg_ss.at[0, 0], neg_rs.at[0, 0], mate)]
        if stage == 6:
            part = neg.at[rows_of(core * 512, 512)]
            return [remote(part, part, neg_ss.at[6, 0], neg_rs.at[6, 0], mate)]
        copies = []
        for d in (1, 2, 3):
            sems = neg_ss.at[stage, d - 1], neg_rs.at[stage, d - 1]
            device, there = ring({1: 0, 2: 1, 3: 2, 4: 1, 5: 0}[stage], d)
            if stage == 1:
                copies.append(remote(n1.at[rows_of(there * 128, 128)], n1r.at[d - 1], *sems, device))
            elif stage == 2:
                copies.append(remote(n2.at[rows_of(there * 32, 32)], n2r.at[d - 1], *sems, device))
            elif stage == 3:
                copies.append(remote(n3, n3r.at[d - 1], *sems, device))
            elif stage == 4:
                copies.append(remote(n4, neg.at[rows_of(block32, 32)], *sems, device))
            else:
                part = neg.at[rows_of(core * 512 + x * 128, 128)]
                copies.append(remote(part, part, *sems, device))
        return copies

    def neg_start(stage):
        if stage == 0:
            n0s[...] = ent_ref[rows_of((1 - core) * 512, 512), :] * mine
        elif stage == 1:
            n1[...] = ent_ref[rows_of(core * 512, 512), :] * mine + n0r[...]
        elif stage == 2:
            n2[...] = n1[rows_of(x * 128, 128), :] + n1r[0] + n1r[1] + n1r[2]
        elif stage == 3:
            n3[...] = n2[rows_of(y * 32, 32), :] + n2r[0] + n2r[1] + n2r[2]
        elif stage == 4:
            total = n3[...] + n3r[0] + n3r[1] + n3r[2]
            n4[...] = total
            neg[rows_of(block32, 32), :] = total
        for copy in neg_copies(stage):
            copy.start()

    def neg_wait(stage):
        for copy in neg_copies(stage):
            copy.wait()

    def rows_copy(j, n, sign):
        return remote(out_rows.at[j, n], in_rows.at[j, n], rows_ss.at[j, n], rows_rs.at[j, n], peer(n, sign, here))

    lane128 = lax.broadcasted_iota(I32, (64, 128), 1)
    lane1024 = lax.broadcasted_iota(I32, (64, NEG), 1).astype(F32)

    def send_rows(j, step):
        hots = []
        for m in range(4):
            _, owner = peer(step * 4 + m, 1, here)
            ids = jnp.sum(jnp.where(lane128 == owner * 4 + j, table_ref[...], 0.0), axis=1, keepdims=True)
            hots.append(jnp.where(lane1024 == ids, 1.0, 0.0).astype(BF))
        rows = jnp.dot(jnp.concatenate(hots, axis=0), ent_ref[...], preferred_element_type=F32).astype(BF)
        out_rows[j, pl.ds(step * 4, 4)] = rows.reshape(4, 64, WIDTH)
        for m in range(4):
            if m == 0:

                @pl.when(step == 0)
                def _():
                    in_rows[j, 0] = rows[0:64]

                @pl.when(step > 0)
                def _():
                    rows_copy(j, step * 4, 1).start()

            else:
                rows_copy(j, step * 4 + m, 1).start()

    def send_steps(first, last):
        def body(i, c):
            send_rows(i // 8, i % 8)
            return c

        lax.fori_loop(first, last, body, 0)

    neg_start(0)
    for stage in range(7):
        send_steps(2 * stage, 2 * stage + 2)
        neg_wait(stage)
        if stage < 6:
            neg_start(stage + 1)
    send_steps(14, 32)
    w_copy.wait()

    nt = (((1,), (1,)), ((), ()))
    tn = (((0,), (0,)), ((), ()))

    def back_copy(j, n, sign):
        return remote(out_back.at[j, n], in_back.at[j, n], back_ss.at[j, n], back_rs.at[j, n], peer(n, sign, here))

    def loss_copy(j, n, sign):
        tile = pl.ds(pl.multiple_of((n // 4) * 128, 128), 128)
        return remote(out_loss.at[j, :, tile], in_loss.at[j, n], loss_ss.at[j, n], loss_rs.at[j, n], peer(n, sign, here))

    def score(j, mb, c):
        for k in range(8):
            if k == 0:

                @pl.when(mb > 0)
                def _():
                    rows_copy(j, mb * 8, -1).wait_recv()

            else:
                rows_copy(j, mb * 8 + k, -1).wait_recv()
        peers = pl.ds(mb * 8, 8)
        h = in_rows[j, peers, 0:32, :].reshape(256, WIDTH)
        t = in_rows[j, peers, 32:64, :].reshape(256, WIDTH).astype(F32)
        q = jnp.dot(h, w16[...], preferred_element_type=F32).astype(BF)
        pos = jnp.sum(q.astype(F32) * t, axis=1, keepdims=True)
        s = lax.dot_general(q, neg[...], nt, preferred_element_type=F32)
        e = jnp.exp(-jnp.abs(s))
        soft = jnp.maximum(s, 0.0) + jnp.log1p(e)
        inv = 1.0 / (1.0 + e)
        coef = (jnp.where(s >= 0.0, inv, e * inv) * (1.0 / NEG)).astype(BF)
        g = jnp.dot(coef, neg[...], preferred_element_type=F32)
        ep = jnp.exp(-jnp.abs(pos))
        loss = jnp.maximum(-pos, 0.0) + jnp.log1p(ep) + jnp.sum(soft, axis=1, keepdims=True) * (1.0 / NEG)
        g = (g - jnp.where(pos <= 0.0, 1.0, ep) / (1.0 + ep) * t).astype(BF)
        gbuf[pl.ds(pl.multiple_of(mb * 256, 256), 256), :] = g
        back = lax.dot_general(g, w16[...], nt, preferred_element_type=F32).astype(BF)
        out_back[j, peers] = back.reshape(8, CAP, WIDTH)
        spot = lax.broadcasted_iota(I32, (256, 128), 1) == 0
        column = jnp.where(spot, loss, 0.0).astype(BF)
        row = lax.dot_general(jnp.ones((16, 128), BF), column, nt, preferred_element_type=F32).astype(BF)
        out_loss[j, :, pl.ds(pl.multiple_of(mb * 256, 256), 256)] = row

        @pl.when(mb == 0)
        def _():
            in_back[j, 0] = back[0:CAP]
            in_loss[j, 0] = row[:, 0:128]

        for k in range(8):
            if k == 0:

                @pl.when(mb > 0)
                def _():
                    back_copy(j, mb * 8, -1).start()
                    loss_copy(j, mb * 8, -1).start()

            else:
                back_copy(j, mb * 8 + k, -1).start()
                loss_copy(j, mb * 8 + k, -1).start()
        return c

    def g1_copy(j):
        return remote(g1s.at[j], g1r.at[j], grp_ss.at[0, j], grp_rs.at[0, j], mate)

    def g2_copy(j):
        return remote(g2s.at[j], g2r.at[j], grp_ss.at[1, j], grp_rs.at[1, j], across)

    def g3_copies(j):
        part = rel_ref.at[j, rows_of(quarter * 128, 128)]
        tile = acc_ref.at[j, quarter]
        return (
            remote(part, part, grp_ss.at[2, j], grp_rs.at[2, j], across),
            remote(tile, tile, grp_ss.at[3, j], grp_rs.at[3, j], across),
        )

    def g4_copies(j):
        part = rel_ref.at[j, rows_of(core * 256, 256)]
        tile = acc_ref.at[j, pl.ds(core * 2, 2)]
        return (
            remote(part, part, grp_ss.at[4, j], grp_rs.at[4, j], mate),
            remote(tile, tile, grp_ss.at[5, j], grp_rs.at[5, j], mate),
        )

    def partial(j):
        for half, mine_too in ((1 - core, False), (core, True)):
            columns = pl.ds(pl.multiple_of(half * 256, 256), 256)
            h = in_rows[j, :, 0:32, columns].reshape(PEERS * CAP, 256)
            value = lax.dot_general(h, gbuf[...], tn, preferred_element_type=F32)
            if mine_too:
                own[j] = value
            else:
                g1s[j] = value.astype(BF)
                g1_copy(j).start()

    def g1_finish(j):
        g1_copy(j).wait_recv()
        other = rows_of((1 - x_hi) * 128, 128)
        g2s[j] = (own[j, other, :] + g1r[j, other, :].astype(F32)).astype(BF)
        g2_copy(j).start()

    def g2_finish(j):
        g2_copy(j).wait_recv()
        keep = rows_of(x_hi * 128, 128)
        total = own[j, keep, :] + g1r[j, keep, :].astype(F32) + g2r[j].astype(F32)
        eye = lax.broadcasted_iota(I32, (128, 128), 0) == lax.broadcasted_iota(I32, (128, 128), 1)
        before = accum_ref[j : j + 1, pl.ds(pl.multiple_of(quarter * 128, 128), 128)]
        before = jnp.sum(jnp.where(eye, before, 0.0), axis=1, keepdims=True)
        after = before + jnp.sum(total * total, axis=1, keepdims=True) * (1.0 / WIDTH)
        rows = rows_of(quarter * 128, 128)
        rel_ref[j, rows, :] = (w32[j, rows, :] - total / jnp.sqrt(after)).astype(BF)
        line = jnp.sum(jnp.where(eye, after, 0.0), axis=0, keepdims=True)
        acc_ref[j, quarter] = jnp.broadcast_to(line, (8, 128))
        for copy in g3_copies(j):
            copy.start()

    def g3_finish(j):
        for copy in g3_copies(j):
            copy.wait_recv()
        for copy in g4_copies(j):
            copy.start()

    def collect(j):
        def arrive(n, c):
            back_copy(j, n, 1).wait_recv()
            loss_copy(j, n, 1).wait_recv()
            return c

        lax.fori_loop(1, PEERS, arrive, 0)
        group = lax.broadcasted_iota(I32, (16, 128), 1) // CAP
        for tile in range(8):
            value = jnp.zeros((16, 128), F32)
            for m in range(4):
                value = jnp.where(group == m, in_loss[j, tile * 4 + m].astype(F32), value)
            lrow[:, tile * 128 : tile * 128 + 128] = value.astype(BF)

        def block(i, c):
            rows = pl.ds(pl.multiple_of(i * 256, 256), 256)
            slot = lax.broadcasted_iota(I32, (256, PEERS * CAP), 1) + j * (PEERS * CAP)
            pick = jnp.where(pos_ref[rows, :] == slot, 1.0, 0.0).astype(BF)
            stack = in_back[j].reshape(PEERS * CAP, WIDTH)
            part = jnp.dot(pick, stack, preferred_element_type=F32).astype(BF)
            losses = lax.dot_general(lrow[...], pick, nt, preferred_element_type=F32)
            if j == 0:
                grad_ref[rows, :] = part
                loss_ref[:, rows] = losses
            else:
                grad_ref[rows, :] = grad_ref[rows, :] + part
                loss_ref[:, rows] = loss_ref[:, rows] + losses
            return c

        lax.fori_loop(0, ROWS // 256, block, 0)

    for j in range(CHUNKS):
        w16[...] = w32[j].astype(BF)
        lax.fori_loop(0, 4, lambda mb, c, j=j: score(j, mb, c), 0)
        partial(j)
        if j >= 1:
            g2_finish(j - 1)
        if j >= 2:
            g3_finish(j - 2)
        if j >= 1:
            collect(j - 1)
        g1_finish(j)
    g3_finish(2)
    g2_finish(3)
    collect(3)
    g3_finish(3)
    for j in range(CHUNKS):
        for copy in g4_copies(j):
            copy.wait_recv()

    def drain(i, c):
        j, n = i // PEERS, i % PEERS

        @pl.when(n > 0)
        def _():
            rows_copy(j, n, 1).wait_send()
            back_copy(j, n, -1).wait_send()
            loss_copy(j, n, -1).wait_send()

        return c

    lax.fori_loop(0, CHUNKS * PEERS, drain, 0)
    for j in range(CHUNKS):
        for copy in (g1_copy(j), g2_copy(j), *g3_copies(j), *g4_copies(j)):
            copy.wait_send()


def per_device(head_ids, relations, tail_ids, neg_owner, entities, rel_weight, rel_accum):
    vmem = pl.BlockSpec(memory_space=pltpu.VMEM)
    table, position = pl.pallas_call(
        prep_kernel,
        out_shape=(jax.ShapeDtypeStruct((64, 128), F32), jax.ShapeDtypeStruct((ROWS, 1), I32)),
        in_specs=[vmem] * 3,
        out_specs=(vmem, vmem),
        name="prep",
    )(relations, head_ids.reshape(ROWS, 1), tail_ids.reshape(ROWS, 1))
    dma = pltpu.SemaphoreType.DMA
    scratch = [
        pltpu.VMEM((CHUNKS, PEERS, 64, WIDTH), BF),
        pltpu.VMEM((CHUNKS, PEERS, 64, WIDTH), BF),
        pltpu.VMEM((CHUNKS, PEERS, CAP, WIDTH), BF),
        pltpu.VMEM((CHUNKS, PEERS, CAP, WIDTH), BF),
        pltpu.VMEM((CHUNKS, 16, PEERS * CAP), BF),
        pltpu.VMEM((CHUNKS, PEERS, 16, 128), BF),
        pltpu.VMEM((CHUNKS, WIDTH, WIDTH), F32),
        pltpu.VMEM((WIDTH, WIDTH), BF),
        pltpu.VMEM((PEERS * CAP, WIDTH), BF),
        pltpu.VMEM((16, PEERS * CAP), BF),
        pltpu.VMEM((CHUNKS, 256, WIDTH), F32),
        pltpu.VMEM((CHUNKS, 256, WIDTH), BF),
        pltpu.VMEM((CHUNKS, 256, WIDTH), BF),
        pltpu.VMEM((CHUNKS, 128, WIDTH), BF),
        pltpu.VMEM((CHUNKS, 128, WIDTH), BF),
        pltpu.VMEM((NEG, WIDTH), BF),
        pltpu.VMEM((512, WIDTH), BF),
        pltpu.VMEM((512, WIDTH), BF),
        pltpu.VMEM((512, WIDTH), BF),
        pltpu.VMEM((3, 128, WIDTH), BF),
        pltpu.VMEM((128, WIDTH), BF),
        pltpu.VMEM((3, 32, WIDTH), BF),
        pltpu.VMEM((32, WIDTH), BF),
        pltpu.VMEM((3, 32, WIDTH), BF),
        pltpu.VMEM((32, WIDTH), BF),
        dma,
        *[dma((CHUNKS, PEERS))] * 6,
        *[dma((7, 3))] * 2,
        *[dma((6, CHUNKS))] * 2,
    ]
    head_grad, losses, new_rel, new_accum = pl.pallas_call(
        main_kernel,
        out_shape=(
            jax.ShapeDtypeStruct((ROWS, WIDTH), BF),
            jax.ShapeDtypeStruct((16, ROWS), F32),
            jax.ShapeDtypeStruct((CHUNKS, WIDTH, WIDTH), BF),
            jax.ShapeDtypeStruct((CHUNKS, 4, 8, 128), F32),
        ),
        in_specs=[pl.BlockSpec(memory_space=pltpu.SMEM), vmem, vmem, vmem, vmem, pl.BlockSpec(memory_space=pl.ANY)],
        out_specs=(vmem,) * 4,
        scratch_shapes=scratch,
        compiler_params=pltpu.CompilerParams(collective_id=0, has_side_effects=True, vmem_limit_bytes=VMEM_BYTES),
        name="rescal",
    )(neg_owner, entities, table, position, rel_accum, rel_weight)
    return (
        losses[0].astype(BF),
        head_grad,
        new_rel.astype(F32),
        new_accum[:, :, 0, :].reshape(CHUNKS, WIDTH),
    )


def solution(mesh):
    placed = (
        P(("grp", "rel")),
        P(("grp", "rel"), None),
        P(("grp", "rel")),
        P(),
        P(("grp", "rel"), None),
        P("rel", None, None),
        P("rel", None),
    )
    return jax.shard_map(
        per_device,
        mesh=mesh,
        in_specs=placed,
        out_specs=(
            P(("grp", "rel")),
            P(("grp", "rel"), None),
            P("rel", None, None),
            P("rel", None),
        ),
        check_vma=False,
    )
```

```python
import jax
import jax.numpy as jnp
from jax import lax
from jax.experimental import pallas as pl
from jax.experimental.pallas import tpu as pltpu
from jax.sharding import PartitionSpec as P

MESH = pl.DeviceIdType.MESH
BF, F32, I32 = jnp.bfloat16, jnp.float32, jnp.int32
ROWS, WIDTH, NEG = 2048, 512, 1024
CHUNKS, SLOTS, CAP = 4, 32, 32
VMEM_BYTES = 61 * 2**20


def place():
    grp, rel = lax.axis_index("grp"), lax.axis_index("rel")
    x_hi, core = grp // 2, grp % 2
    x_lo, y, z = rel // 16, (rel // 4) % 4, rel % 4
    return x_hi, core, x_hi * 2 + x_lo, x_lo, y, z


def device_at(core, x, y, z):
    return ((x // 2) * 2 + core, (x % 2) * 16 + y * 4 + z)


def peer(j, d, sign, here):
    x_hi, core, x, x_lo, y, z = here
    dx, dm, odd = d % 2, d // 2, j % 2
    x = (x + dx * (1 + 2 * (x % 2) + 2 * (dm % 2))) % 4
    return device_at(core, x, (y + sign * dm * odd + 4) % 4, (z + sign * dm * (1 - odd) + 4) % 4)


def make_table(rel_ref, head_ref, tail_ref, table, pos, spots, here):
    x_hi, core, x, x_lo, y, z = here
    line = lax.broadcasted_iota(I32, (128, 128), 0)
    lane = lax.broadcasted_iota(I32, (128, 128), 1)
    earlier = jnp.where(line < lane, 1.0, 0.0).astype(BF)
    seen = jnp.zeros((128, 1), F32)
    total = jnp.zeros((128, 128), F32)
    for i in range(ROWS // 128):
        rel, head, tail = rel_ref[i : i + 1, :], head_ref[i : i + 1, :] + 1, tail_ref[i : i + 1, :] + 1
        hot = jnp.where(line == rel, 1.0, 0.0)
        before = jnp.dot(hot.astype(BF), earlier, preferred_element_type=F32) + seen
        rank = jnp.sum(hot * before, axis=0, keepdims=True).astype(I32)
        digit = jnp.where(line < 64, jnp.where(line < 32, head // 32, head % 32), jnp.where(line < 96, tail // 32, tail % 32))
        marks = jnp.where(line % 32 == rank, digit, 0).astype(F32).astype(BF)
        total = total + lax.dot_general(marks, hot.astype(BF), (((1,), (1,)), ((), ())), preferred_element_type=F32)
        seen = seen + jnp.sum(hot, axis=1, keepdims=True)
        owner = rel // 4
        dy, dz = (owner // 4 % 4 + 4 - y) % 4, (owner % 4 + 4 - z) % 4
        dx, odd = (owner // 16 + 2 - x_lo) % 2, rel % 2
        dm, dk = dy * odd + dz * (1 - odd), dz * odd + dy * (1 - odd)
        spot = (rel % 4) * (SLOTS * CAP) + (dk * 8 + dm * 2 + dx) * CAP + rank
        spots[i : i + 1, :] = spot
        pos[i * 128 : i * 128 + 128, :] = jnp.sum(jnp.where(line == lane, spot, 0), axis=1, keepdims=True)
    table[0:32, :] = total[0:32] * 32.0 + total[32:64] - 1.0
    table[32:64, :] = total[64:96] * 32.0 + total[96:128] - 1.0


def main_kernel(
    owner_ref, ent_ref, relation_ref, head_ref, tail_ref, accum_ref, weight_ref,
    grad_ref, loss_ref, new_ref, acc_out,
    table_ref, pos_ref, spots, rel_ref, acc_ref,
    out_rows, in_rows, out_back, in_back, out_loss, in_loss, w32, w16,
    own, g1s, g1r, gys, gyr, g2s, g2r,
    neg, n0s, n0r, n1, n1r, n2, n2r, n3, n3r, n4,
    w_sem, new_sem, rows_ss, rows_rs, back_ss, back_rs, loss_ss, loss_rs,
    wr_ss, wr_rs, wm_ss, wm_rs, g1_ss, g1_rs, gy_ss, gy_rs, neg_ss, neg_rs, grp_ss, grp_rs,
):
    here = place()
    x_hi, core, x, x_lo, y, z = here
    me = lax.axis_index("grp") * 32 + lax.axis_index("rel")
    mate = device_at(1 - core, x, y, z)
    across = device_at(core, (x + 2) % 4, y, z)
    beside = device_at(core, (x + 3 + 2 * (x % 2)) % 4, y, z)

    def remote(src, dst, ss, rs, device):
        return pltpu.make_async_remote_copy(src_ref=src, dst_ref=dst, send_sem=ss, recv_sem=rs, device_id=device, device_id_type=MESH)

    w_copy = pltpu.make_async_copy(weight_ref, w32, w_sem)
    w_copy.start()

    barrier = pltpu.get_barrier_semaphore()

    def greet(device):
        pl.semaphore_signal(barrier, inc=1, device_id=device, device_id_type=MESH)

    for d in range(1, 8):
        greet(peer(0, d, 1, here))
    for d in range(2, 8):
        greet(peer(1, d, 1, here))
    for device in (mate, across, beside):
        greet(device)
    out_loss[...] = jnp.zeros_like(out_loss)
    w_copy.wait()
    for j in range(2):
        w16[j, 0] = w32[j].astype(BF)
    pl.semaphore_wait(barrier, 16)

    mine = (owner_ref[0] == me).astype(F32).astype(BF)

    def ring(axis, d):
        if axis == 0:
            return device_at(core, (x + d) % 4, y, z), (x + d) % 4
        if axis == 1:
            return device_at(core, x, (y + d) % 4, z), (y + d) % 4
        return device_at(core, x, y, (z + d) % 4), (z + d) % 4

    def rows_of(start, size):
        return pl.ds(pl.multiple_of(start, size), size)

    block32 = core * 512 + x * 128 + y * 32

    def neg_copies(stage):
        if stage == 0:
            return [remote(n0s, n0r, neg_ss.at[0, 0], neg_rs.at[0, 0], mate)]
        if stage == 6:
            part = neg.at[rows_of(core * 512, 512)]
            return [remote(part, part, neg_ss.at[6, 0], neg_rs.at[6, 0], mate)]
        copies = []
        for d in (1, 2, 3):
            sems = neg_ss.at[stage, d - 1], neg_rs.at[stage, d - 1]
            device, there = ring({1: 0, 2: 1, 3: 2, 4: 1, 5: 0}[stage], d)
            if stage == 1:
                copies.append(remote(n1.at[rows_of(there * 128, 128)], n1r.at[d - 1], *sems, device))
            elif stage == 2:
                copies.append(remote(n2.at[rows_of(there * 32, 32)], n2r.at[d - 1], *sems, device))
            elif stage == 3:
                copies.append(remote(n3, n3r.at[d - 1], *sems, device))
            elif stage == 4:
                copies.append(remote(n4, neg.at[rows_of(block32, 32)], *sems, device))
            else:
                part = neg.at[rows_of(core * 512 + x * 128, 128)]
                copies.append(remote(part, part, *sems, device))
        return copies

    def neg_start(stage):
        if stage == 0:
            n0s[...] = ent_ref[rows_of((1 - core) * 512, 512), :] * mine
        elif stage == 1:
            n1[...] = ent_ref[rows_of(core * 512, 512), :] * mine + n0r[...]
        elif stage == 2:
            n2[...] = n1[rows_of(x * 128, 128), :] + n1r[0] + n1r[1] + n1r[2]
        elif stage == 3:
            n3[...] = n2[rows_of(y * 32, 32), :] + n2r[0] + n2r[1] + n2r[2]
        elif stage == 4:
            total = n3[...] + n3r[0] + n3r[1] + n3r[2]
            n4[...] = total
            neg[rows_of(block32, 32), :] = total
        for copy in neg_copies(stage):
            copy.start()

    def neg_wait(stage):
        for copy in neg_copies(stage):
            copy.wait()

    def rows_copy(j, n, sign):
        return remote(out_rows.at[j % 2, n], in_rows.at[j, n], rows_ss.at[j, n], rows_rs.at[j, n], peer(j, n % 8, sign, here))

    lane128 = lax.broadcasted_iota(I32, (64, 128), 1)
    lane1024 = lax.broadcasted_iota(I32, (64, NEG), 1).astype(F32)

    def send_rows(pair, i):
        j, odd = 2 * pair + i % 2, i % 2
        k = (i // 4 + pair) % 4
        first = k * 8 + (i // 2 % 2) * 4
        hots = []
        for m in range(4):
            d = (first + m) % 8
            dm = d // 2
            oy = (y + dm * odd + k * (1 - odd)) % 4
            oz = (z + dm * (1 - odd) + k * odd) % 4
            owner = ((x_lo + d) % 2) * 16 + oy * 4 + oz
            ids = jnp.sum(jnp.where(lane128 == owner * 4 + j, table_ref[...], 0.0), axis=1, keepdims=True)
            hots.append(jnp.where(lane1024 == ids, 1.0, 0.0).astype(BF))
        rows = jnp.dot(jnp.concatenate(hots, axis=0), ent_ref[...], preferred_element_type=F32).astype(BF)
        local = i // 2 % 2 == 0
        for m in range(4):
            if pair > 0:
                if m == 0:

                    @pl.when(jnp.logical_not(local))
                    def _():
                        rows_copy(j - 2, first, 1).wait_send()

                else:
                    rows_copy(j - 2, first + m, 1).wait_send()
        out_rows[j % 2, pl.ds(first, 4)] = rows.reshape(4, 64, WIDTH)
        for m in range(4):
            if m == 0:

                @pl.when(local)
                def _():
                    in_rows[j, first] = rows[0:64]

                @pl.when(jnp.logical_not(local))
                def _():
                    rows_copy(j, first, 1).start()

            else:
                rows_copy(j, first + m, 1).start()

    def send_steps(pair, first, last):
        def body(i, c):
            send_rows(pair, i)
            return c

        lax.fori_loop(first, last, body, 0)

    my_half = rows_of(core * 256, 256)

    def w_ring(j, k):
        device = device_at(core, x, (y + (4 - k) * (1 - j % 2)) % 4, (z + (4 - k) * (j % 2)) % 4)
        return remote(w16.at[j, 0, my_half], w16.at[j, k, my_half], wr_ss.at[j, k], wr_rs.at[j, k], device)

    def w_mate(j, k):
        part = w16.at[j, k, my_half]
        return remote(part, part, wm_ss.at[j, k], wm_rs.at[j, k], mate)

    def w_send(j):
        for k in (1, 2, 3):
            w_ring(j, k).start()

    def w_forward(j):
        for k in (1, 2, 3):
            w_ring(j, k).wait_recv()
            w_mate(j, k).start()

    w_send(0)
    w_send(1)
    neg_start(0)
    make_table(relation_ref, head_ref, tail_ref, table_ref, pos_ref, spots, here)
    at = 0
    for stage, to in enumerate((3, 6, 9, 12, 14, 16)):
        send_steps(0, at, to)
        at = to
        neg_wait(stage)
        neg_start(stage + 1)
    w_forward(0)
    w_forward(1)
    for j in (2, 3):
        w16[j, 0] = w32[j].astype(BF)
        w_send(j)
    send_steps(1, 0, 4)
    neg_wait(6)

    nt = (((1,), (1,)), ((), ()))
    tn = (((0,), (0,)), ((), ()))

    def back_copy(j, n, sign):
        return remote(out_back.at[j % 2, n], in_back.at[j, n], back_ss.at[j, n], back_rs.at[j, n], peer(j, n % 8, sign, here))

    def loss_copy(odd, d, sign):
        return remote(out_loss.at[odd, d // 4], in_loss.at[odd, d], loss_ss.at[odd, d], loss_rs.at[odd, d], peer(odd, d, sign, here))

    def score(j, i, c):
        k = (i + j // 2) % 4
        first = k * 8
        for d in range(1, 8):
            rows_copy(j, first + d, -1).wait_recv()
        slots = pl.ds(first, 8)
        h = in_rows[j, slots, 0:32, :].reshape(256, WIDTH)
        t = in_rows[j, slots, 32:64, :].reshape(256, WIDTH).astype(F32)
        w = w16.at[j, k]
        q = jnp.dot(h, w[...], preferred_element_type=F32).astype(BF)
        pos = jnp.sum(q.astype(F32) * t, axis=1, keepdims=True)
        s = lax.dot_general(q, neg[...], nt, preferred_element_type=F32)
        e = jnp.exp(-jnp.abs(s))
        soft = jnp.maximum(s, 0.0) + jnp.log1p(e)
        inv = 1.0 / (1.0 + e)
        coef = (jnp.where(s >= 0.0, inv, e * inv) * (1.0 / NEG)).astype(BF)
        g = jnp.dot(coef, neg[...], preferred_element_type=F32)
        ep = jnp.exp(-jnp.abs(pos))
        loss = jnp.maximum(-pos, 0.0) + jnp.log1p(ep) + jnp.sum(soft, axis=1, keepdims=True) * (1.0 / NEG)
        g = (g - jnp.where(pos <= 0.0, 1.0, ep) / (1.0 + ep) * t).astype(BF)
        back = lax.dot_general(g, w[...], nt, preferred_element_type=F32).astype(BF)
        if j >= 2:
            for d in range(1, 8):
                back_copy(j - 2, first + d, -1).wait_send()
        out_back[j % 2, slots] = back.reshape(8, CAP, WIDTH)
        for d in range(1, 8):
            back_copy(j, first + d, -1).start()
        in_back[j, first] = back[0:CAP]
        spot = lax.broadcasted_iota(I32, (256, 128), 1) == 0
        column = jnp.where(spot, loss, 0.0).astype(BF)
        row = lax.dot_general(jnp.ones((16, 128), BF), column, nt, preferred_element_type=F32).astype(BF)
        line = lax.broadcasted_iota(I32, (16, 128), 0) == (j // 2) * 4 + k
        for half in range(2):
            out_loss[j % 2, half] = jnp.where(line, row[:, half * 128 : half * 128 + 128], out_loss[j % 2, half])

        def outer(half):
            columns = pl.ds(pl.multiple_of(half * 256, 256), 256)
            return lax.dot_general(in_rows[j, slots, 0:32, columns].reshape(256, 256), g, tn, preferred_element_type=F32)

        if j >= 2:
            g1_copy(j - 2, k).wait_send()
        g1s[j % 2, k] = outer(1 - core).astype(BF)
        g1_copy(j, k).start()
        value = outer(core)

        @pl.when(k == 0)
        def _():
            own[j] = value

        @pl.when(k > 0)
        def _():
            if j >= 2:
                gy_copy(j - 2, k).wait_send()
            gys[j % 2, k] = value.astype(BF)

        @pl.when(i > 0)
        def _():
            g1_finish(j, (i - 1 + j // 2) % 4)

        return c

    def g1_copy(j, k):
        return remote(g1s.at[j % 2, k], g1r.at[j, k], g1_ss.at[j, k], g1_rs.at[j, k], mate)

    def gy_copy(j, k):
        device = device_at(core, x, (y + k * (1 - j % 2)) % 4, (z + k * (j % 2)) % 4)
        return remote(gys.at[j % 2, k], gyr.at[j, k], gy_ss.at[j, k], gy_rs.at[j, k], device)

    def g1_finish(j, k):
        g1_copy(j, k).wait_recv()

        @pl.when(k == 0)
        def _():
            own[j] = own[j] + g1r[j, 0].astype(F32)

        @pl.when(k > 0)
        def _():
            gys[j % 2, k] = (gys[j % 2, k].astype(F32) + g1r[j, k].astype(F32)).astype(BF)
            gy_copy(j, k).start()

    def gy_finish(j):
        for k in (1, 2, 3):
            gy_copy(j, k).wait_recv()
        own[j] = own[j] + gyr[j, 1].astype(F32) + gyr[j, 2].astype(F32) + gyr[j, 3].astype(F32)
        g2s[j] = own[j].astype(BF)
        g2_copy(j).start()

    def g2_copy(j):
        return remote(g2s.at[j], g2r.at[j], grp_ss.at[1, j], grp_rs.at[1, j], across)

    def g4_copies(j):
        part = rel_ref.at[j, rows_of(core * 256, 256)]
        tile = acc_ref.at[j, pl.ds(core * 2, 2)]
        return (
            remote(part, part, grp_ss.at[4, j], grp_rs.at[4, j], mate),
            remote(tile, tile, grp_ss.at[5, j], grp_rs.at[5, j], mate),
        )

    def g2_finish(j):
        g2_copy(j).wait_recv()
        eye = lax.broadcasted_iota(I32, (128, 128), 0) == lax.broadcasted_iota(I32, (128, 128), 1)
        for part in range(2):
            here_rows = slice(part * 128, part * 128 + 128)
            total = g2s[j, here_rows, :].astype(F32) + g2r[j, here_rows, :].astype(F32)
            quarter = core * 2 + part
            before = accum_ref[j : j + 1, pl.ds(pl.multiple_of(quarter * 128, 128), 128)]
            before = jnp.sum(jnp.where(eye, before, 0.0), axis=1, keepdims=True)
            after = before + jnp.sum(total * total, axis=1, keepdims=True) * (1.0 / WIDTH)
            rows = rows_of(quarter * 128, 128)
            rel_ref[j, rows, :] = (w32[j, rows, :] - total / jnp.sqrt(after)).astype(BF)
            line = jnp.sum(jnp.where(eye, after, 0.0), axis=0, keepdims=True)
            acc_ref[j, quarter] = jnp.broadcast_to(line, (8, 128))
        for copy in g4_copies(j):
            copy.start()

    def collect_wait(j):
        for n in range(SLOTS):
            if n % 8 > 0:
                back_copy(j, n, 1).wait_recv()

    def collect(j, first, last):
        def block(i, c):
            rows = pl.ds(pl.multiple_of(i * 256, 256), 256)
            slot = lax.broadcasted_iota(I32, (256, SLOTS * CAP), 1) + j * (SLOTS * CAP)
            pick = jnp.where(pos_ref[rows, :] == slot, 1.0, 0.0).astype(BF)
            stack = in_back[j].reshape(SLOTS * CAP, WIDTH)
            part = jnp.dot(pick, stack, preferred_element_type=F32).astype(BF)
            if j == 0:
                grad_ref[rows, :] = part
            else:
                grad_ref[rows, :] = grad_ref[rows, :] + part
            return c

        lax.fori_loop(first, last, block, 0)

    def send_losses():
        for odd in range(2):
            in_loss[odd, 0] = out_loss[odd, 0]
            for d in range(1, 8):
                loss_copy(odd, d, -1).start()

    def collect_losses():
        group = lax.broadcasted_iota(I32, (16, 128), 1) // CAP
        tiles = []
        for odd in range(2):
            for half in range(2):
                value = jnp.zeros((16, 128), F32)
                for m in range(4):
                    if half + m > 0:
                        loss_copy(odd, half * 4 + m, 1).wait_recv()
                    value = jnp.where(group == m, in_loss[odd, half * 4 + m].astype(F32), value)
                tiles.append(value)
        stack = jnp.concatenate(tiles, axis=0).astype(BF)
        line = lax.broadcasted_iota(I32, (64, 128), 0)
        full = lax.broadcasted_iota(I32, (128, 128), 0)
        for i in range(ROWS // 128):
            spot = spots[i : i + 1, :]
            j = spot // 1024
            row = (j % 2) * 32 + (spot // 128 % 2) * 16 + (j // 2) * 4 + spot // 256 % 4
            pick = jnp.where(line == row, 1.0, 0.0).astype(BF)
            found = lax.dot_general(stack, pick, tn, preferred_element_type=F32)
            loss_ref[i : i + 1, :] = jnp.sum(jnp.where(full == spot % 128, found, 0.0), axis=0, keepdims=True)

    def g4_finish(j):
        for copy in g4_copies(j):
            copy.wait_recv()
        for q in range(4):
            acc_out[j : j + 1, q * 128 : q * 128 + 128] = acc_ref[j, q, 0:1]
        w32[j] = rel_ref[j].astype(F32)
        pltpu.make_async_copy(w32.at[j], new_ref.at[j], new_sem.at[j]).start()

    for j in range(CHUNKS):
        for k in (1, 2, 3):
            w_mate(j, k).wait_recv()
        if j == 0:

            def mixed(i, c):
                score(0, i, c)

                @pl.when(i < 3)
                def _():
                    send_steps(1, i * 4 + 4, i * 4 + 8)

                return c

            lax.fori_loop(0, 4, mixed, 0)
            w_forward(2)
            w_forward(3)
        else:
            lax.fori_loop(0, 4, lambda i, c, j=j: score(j, i, c), 0)
        if j == CHUNKS - 1:
            send_losses()
        g1_finish(j, (3 + j // 2) % 4)
        if j >= 1:
            gy_finish(j - 1)
        if j >= 2:
            g2_finish(j - 2)
        if j >= 3:
            g4_finish(j - 3)
        if j >= 1:
            collect_wait(j - 1)
            collect(j - 1, 0, 8)
    g2_finish(2)
    g4_finish(1)
    gy_finish(3)
    collect_wait(3)
    collect(3, 0, 4)
    g2_finish(3)
    g4_finish(2)
    collect(3, 4, 8)
    collect_losses()
    g4_finish(3)

    for j in range(CHUNKS):
        for k in (1, 2, 3):
            w_ring(j, k).wait_send()
            w_mate(j, k).wait_send()
        if j >= 2:
            for n in range(SLOTS):
                if n % 8 > 0:
                    rows_copy(j, n, 1).wait_send()
                    back_copy(j, n, -1).wait_send()
            for k in range(4):
                g1_copy(j, k).wait_send()
            for k in (1, 2, 3):
                gy_copy(j, k).wait_send()
        for copy in (g2_copy(j), *g4_copies(j)):
            copy.wait_send()
        pltpu.make_async_copy(w32.at[j], new_ref.at[j], new_sem.at[j]).wait()
    for odd in range(2):
        for d in range(1, 8):
            loss_copy(odd, d, -1).wait_send()


def per_device(head_ids, relations, tail_ids, neg_owner, entities, rel_weight, rel_accum):
    vmem, anywhere = pl.BlockSpec(memory_space=pltpu.VMEM), pl.BlockSpec(memory_space=pl.ANY)
    tiles = (ROWS // 128, 128)
    dma = pltpu.SemaphoreType.DMA
    scratch = [
        pltpu.VMEM((64, 128), F32),
        pltpu.VMEM((ROWS, 1), I32),
        pltpu.VMEM((16, 128), I32),
        pltpu.VMEM((CHUNKS, WIDTH, WIDTH), BF),
        pltpu.VMEM((CHUNKS, 4, 8, 128), F32),
        pltpu.VMEM((2, SLOTS, 64, WIDTH), BF),
        pltpu.VMEM((CHUNKS, SLOTS, 64, WIDTH), BF),
        pltpu.VMEM((2, SLOTS, CAP, WIDTH), BF),
        pltpu.VMEM((CHUNKS, SLOTS, CAP, WIDTH), BF),
        pltpu.VMEM((2, 2, 16, 128), BF),
        pltpu.VMEM((2, 8, 16, 128), BF),
        pltpu.VMEM((CHUNKS, WIDTH, WIDTH), F32),
        pltpu.VMEM((CHUNKS, 4, WIDTH, WIDTH), BF),
        pltpu.VMEM((CHUNKS, 256, WIDTH), F32),
        pltpu.VMEM((2, 4, 256, WIDTH), BF),
        pltpu.VMEM((CHUNKS, 4, 256, WIDTH), BF),
        pltpu.VMEM((2, 4, 256, WIDTH), BF),
        pltpu.VMEM((CHUNKS, 4, 256, WIDTH), BF),
        pltpu.VMEM((CHUNKS, 256, WIDTH), BF),
        pltpu.VMEM((CHUNKS, 256, WIDTH), BF),
        pltpu.VMEM((NEG, WIDTH), BF),
        pltpu.VMEM((512, WIDTH), BF),
        pltpu.VMEM((512, WIDTH), BF),
        pltpu.VMEM((512, WIDTH), BF),
        pltpu.VMEM((3, 128, WIDTH), BF),
        pltpu.VMEM((128, WIDTH), BF),
        pltpu.VMEM((3, 32, WIDTH), BF),
        pltpu.VMEM((32, WIDTH), BF),
        pltpu.VMEM((3, 32, WIDTH), BF),
        pltpu.VMEM((32, WIDTH), BF),
        dma,
        dma((CHUNKS,)),
        *[dma((CHUNKS, SLOTS))] * 4,
        *[dma((2, 8))] * 2,
        *[dma((CHUNKS, 4))] * 8,
        *[dma((7, 3))] * 2,
        *[dma((6, CHUNKS))] * 2,
    ]
    head_grad, losses, new_rel, new_accum = pl.pallas_call(
        main_kernel,
        out_shape=(
            jax.ShapeDtypeStruct((ROWS, WIDTH), BF),
            jax.ShapeDtypeStruct((16, 128), F32),
            jax.ShapeDtypeStruct((CHUNKS, WIDTH, WIDTH), F32),
            jax.ShapeDtypeStruct((CHUNKS, WIDTH), F32),
        ),
        in_specs=[pl.BlockSpec(memory_space=pltpu.SMEM), *[vmem] * 5, anywhere],
        out_specs=(vmem, vmem, anywhere, vmem),
        scratch_shapes=scratch,
        compiler_params=pltpu.CompilerParams(collective_id=0, has_side_effects=True, vmem_limit_bytes=VMEM_BYTES),
        name="rescal",
    )(neg_owner, entities, relations.reshape(tiles), head_ids.reshape(tiles), tail_ids.reshape(tiles), rel_accum, rel_weight)
    return losses.reshape(ROWS).astype(BF), head_grad, new_rel, new_accum


def solution(mesh):
    placed = (
        P(("grp", "rel")),
        P(("grp", "rel"), None),
        P(("grp", "rel")),
        P(),
        P(("grp", "rel"), None),
        P("rel", None, None),
        P("rel", None),
    )
    return jax.shard_map(
        per_device,
        mesh=mesh,
        in_specs=placed,
        out_specs=(
            P(("grp", "rel")),
            P(("grp", "rel"), None),
            P("rel", None, None),
            P("rel", None),
        ),
        check_vma=False,
    )
```

```python
import jax
import jax.numpy as jnp
from jax import lax
from jax.experimental import pallas as pl
from jax.experimental.pallas import tpu as pltpu
from jax.sharding import PartitionSpec as P

MESH = pl.DeviceIdType.MESH
BF, F32, I32 = jnp.bfloat16, jnp.float32, jnp.int32
ROWS, WIDTH, NEG = 2048, 512, 1024
CHUNKS, SLOTS, CAP = 4, 32, 32
VMEM_BYTES = 61 * 2**20


def place():
    grp, rel = lax.axis_index("grp"), lax.axis_index("rel")
    x_hi, core = grp // 2, grp % 2
    x_lo, y, z = rel // 16, (rel // 4) % 4, rel % 4
    return x_hi, core, x_hi * 2 + x_lo, x_lo, y, z


def device_at(core, x, y, z):
    return ((x // 2) * 2 + core, (x % 2) * 16 + y * 4 + z)


def peer(j, d, sign, here):
    x_hi, core, x, x_lo, y, z = here
    dx, dm, odd = d % 2, d // 2, j % 2
    x = (x + dx * (1 + 2 * (x % 2) + 2 * (dm % 2))) % 4
    return device_at(core, x, (y + sign * dm * odd + 4) % 4, (z + sign * dm * (1 - odd) + 4) % 4)


def make_table(rel_ref, head_ref, tail_ref, table, pos, spots, here):
    x_hi, core, x, x_lo, y, z = here
    line = lax.broadcasted_iota(I32, (128, 128), 0)
    lane = lax.broadcasted_iota(I32, (128, 128), 1)
    earlier = jnp.where(line < lane, 1.0, 0.0).astype(BF)
    seen = jnp.zeros((128, 1), F32)
    total = jnp.zeros((128, 128), F32)
    for i in range(ROWS // 128):
        rel, head, tail = rel_ref[i : i + 1, :], head_ref[i : i + 1, :] + 1, tail_ref[i : i + 1, :] + 1
        hot = jnp.where(line == rel, 1.0, 0.0)
        before = jnp.dot(hot.astype(BF), earlier, preferred_element_type=F32) + seen
        rank = jnp.sum(hot * before, axis=0, keepdims=True).astype(I32)
        digit = jnp.where(line < 64, jnp.where(line < 32, head // 32, head % 32), jnp.where(line < 96, tail // 32, tail % 32))
        marks = jnp.where(line % 32 == rank, digit, 0).astype(F32).astype(BF)
        total = total + lax.dot_general(marks, hot.astype(BF), (((1,), (1,)), ((), ())), preferred_element_type=F32)
        seen = seen + jnp.sum(hot, axis=1, keepdims=True)
        owner = rel // 4
        dy, dz = (owner // 4 % 4 + 4 - y) % 4, (owner % 4 + 4 - z) % 4
        dx, odd = (owner // 16 + 2 - x_lo) % 2, rel % 2
        dm, dk = dy * odd + dz * (1 - odd), dz * odd + dy * (1 - odd)
        spot = (rel % 4) * (SLOTS * CAP) + (dk * 8 + dm * 2 + dx) * CAP + rank
        spots[i : i + 1, :] = spot
        pos[i * 128 : i * 128 + 128, :] = jnp.sum(jnp.where(line == lane, spot, 0), axis=1, keepdims=True)
    table[0:32, :] = total[0:32] * 32.0 + total[32:64] - 1.0
    table[32:64, :] = total[64:96] * 32.0 + total[96:128] - 1.0


def main_kernel(
    owner_ref, ent_ref, relation_ref, head_ref, tail_ref, accum_ref, weight_ref,
    grad_out, loss_ref, new_ref, acc_out,
    grad_ref,    table_ref, pos_ref, spots, rel_ref, acc_ref,
    out_rows, in_rows, out_back, in_back, out_loss, in_loss, w32, w16,
    own, g1s, g1r, gys, gyr, g2s, g2r,
    neg, n0s, n0r, n1, n1r, n2, n2r, n3, n3r, n4,
    w_sem, new_sem, grad_sem, rows_ss, rows_rs, back_ss, back_rs, loss_ss, loss_rs,
    wr_ss, wr_rs, wm_ss, wm_rs, g1_ss, g1_rs, gy_ss, gy_rs, neg_ss, neg_rs, grp_ss, grp_rs,
):
    here = place()
    x_hi, core, x, x_lo, y, z = here
    me = lax.axis_index("grp") * 32 + lax.axis_index("rel")
    mate = device_at(1 - core, x, y, z)
    across = device_at(core, (x + 2) % 4, y, z)
    beside = device_at(core, (x + 3 + 2 * (x % 2)) % 4, y, z)

    def remote(src, dst, ss, rs, device):
        return pltpu.make_async_remote_copy(src_ref=src, dst_ref=dst, send_sem=ss, recv_sem=rs, device_id=device, device_id_type=MESH)

    w_copies = [pltpu.make_async_copy(weight_ref.at[j], w32.at[j], w_sem.at[j]) for j in range(CHUNKS)]
    for copy in w_copies:
        copy.start()

    barrier = pltpu.get_barrier_semaphore()

    def greet(device):
        pl.semaphore_signal(barrier, inc=1, device_id=device, device_id_type=MESH)

    for d in range(1, 8):
        greet(peer(0, d, 1, here))
    for d in range(2, 8):
        greet(peer(1, d, 1, here))
    for device in (mate, across, beside):
        greet(device)
    out_loss[...] = jnp.zeros_like(out_loss)
    for j in range(2):
        w_copies[j].wait()
        w16[j, 0] = w32[j].astype(BF)
    pl.semaphore_wait(barrier, 16)

    mine = (owner_ref[0] == me).astype(F32).astype(BF)

    def ring(axis, d):
        if axis == 0:
            return device_at(core, (x + d) % 4, y, z), (x + d) % 4
        if axis == 1:
            return device_at(core, x, (y + d) % 4, z), (y + d) % 4
        return device_at(core, x, y, (z + d) % 4), (z + d) % 4

    def rows_of(start, size):
        return pl.ds(pl.multiple_of(start, size), size)

    block32 = core * 512 + x * 128 + y * 32

    def neg_copies(stage):
        if stage == 0:
            return [remote(n0s, n0r, neg_ss.at[0, 0], neg_rs.at[0, 0], mate)]
        if stage == 6:
            part = neg.at[rows_of(core * 512, 512)]
            return [remote(part, part, neg_ss.at[6, 0], neg_rs.at[6, 0], mate)]
        copies = []
        for d in (1, 2, 3):
            sems = neg_ss.at[stage, d - 1], neg_rs.at[stage, d - 1]
            device, there = ring({1: 0, 2: 1, 3: 2, 4: 1, 5: 0}[stage], d)
            if stage == 1:
                copies.append(remote(n1.at[rows_of(there * 128, 128)], n1r.at[d - 1], *sems, device))
            elif stage == 2:
                copies.append(remote(n2.at[rows_of(there * 32, 32)], n2r.at[d - 1], *sems, device))
            elif stage == 3:
                copies.append(remote(n3, n3r.at[d - 1], *sems, device))
            elif stage == 4:
                copies.append(remote(n4, neg.at[rows_of(block32, 32)], *sems, device))
            else:
                part = neg.at[rows_of(core * 512 + x * 128, 128)]
                copies.append(remote(part, part, *sems, device))
        return copies

    def neg_start(stage):
        if stage == 0:
            n0s[...] = ent_ref[rows_of((1 - core) * 512, 512), :] * mine
        elif stage == 1:
            n1[...] = ent_ref[rows_of(core * 512, 512), :] * mine + n0r[...]
        elif stage == 2:
            n2[...] = n1[rows_of(x * 128, 128), :] + n1r[0] + n1r[1] + n1r[2]
        elif stage == 3:
            n3[...] = n2[rows_of(y * 32, 32), :] + n2r[0] + n2r[1] + n2r[2]
        elif stage == 4:
            total = n3[...] + n3r[0] + n3r[1] + n3r[2]
            n4[...] = total
            neg[rows_of(block32, 32), :] = total
        for copy in neg_copies(stage):
            copy.start()

    def neg_wait(stage):
        for copy in neg_copies(stage):
            copy.wait()

    def rows_copy(j, n, sign):
        return remote(out_rows.at[j % 2, n], in_rows.at[j, n], rows_ss.at[j, n], rows_rs.at[j, n], peer(j, n % 8, sign, here))

    lane128 = lax.broadcasted_iota(I32, (64, 128), 1)
    lane1024 = lax.broadcasted_iota(I32, (64, NEG), 1).astype(F32)

    def send_rows(pair, i):
        j, odd = 2 * pair + i % 2, i % 2
        k = (i // 4 + 2 * pair) % 4
        first = k * 8 + (i // 2 % 2) * 4
        hots = []
        for m in range(4):
            d = (first + m) % 8
            dm = d // 2
            oy = (y + dm * odd + k * (1 - odd)) % 4
            oz = (z + dm * (1 - odd) + k * odd) % 4
            owner = ((x_lo + d) % 2) * 16 + oy * 4 + oz
            ids = jnp.sum(jnp.where(lane128 == owner * 4 + j, table_ref[...], 0.0), axis=1, keepdims=True)
            hots.append(jnp.where(lane1024 == ids, 1.0, 0.0).astype(BF))
        rows = jnp.dot(jnp.concatenate(hots, axis=0), ent_ref[...], preferred_element_type=F32).astype(BF)
        local = i // 2 % 2 == 0
        for m in range(4):
            if pair > 0:
                if m == 0:

                    @pl.when(jnp.logical_not(local))
                    def _():
                        rows_copy(j - 2, first, 1).wait_send()

                else:
                    rows_copy(j - 2, first + m, 1).wait_send()
        out_rows[j % 2, pl.ds(first, 4)] = rows.reshape(4, 64, WIDTH)
        for m in range(4):
            if m == 0:

                @pl.when(local)
                def _():
                    in_rows[j, first] = rows[0:64]

                @pl.when(jnp.logical_not(local))
                def _():
                    rows_copy(j, first, 1).start()

            else:
                rows_copy(j, first + m, 1).start()

    def send_steps(pair, first, last):
        def body(i, c):
            send_rows(pair, i)
            return c

        lax.fori_loop(first, last, body, 0)

    my_half = rows_of(core * 256, 256)

    def w_ring(j, k):
        device = device_at(core, x, (y + (4 - k) * (1 - j % 2)) % 4, (z + (4 - k) * (j % 2)) % 4)
        return remote(w16.at[j, 0, my_half], w16.at[j, k, my_half], wr_ss.at[j, k], wr_rs.at[j, k], device)

    def w_mate(j, k):
        part = w16.at[j, k, my_half]
        return remote(part, part, wm_ss.at[j, k], wm_rs.at[j, k], mate)

    def w_relay(j, k):
        part = rows_of(core * 256 + (k // 2) * 128, 128)
        device = device_at(core, x, (y + (4 - k) * (1 - j % 2)) % 4, (z + (4 - k) * (j % 2)) % 4)
        return remote(w16.at[j, k, part], w16.at[j, 2, part], wr_ss.at[j, k - 1], wr_rs.at[j, k - 1], device)

    def w_send(j):
        for k in (1, 3):
            w_ring(j, k).start()

    def w_pass(j):
        for k in (1, 3):
            w_ring(j, k).wait_recv()
            w_relay(j, k).start()
            w_mate(j, k).start()

    def w_forward(j):
        for k in (1, 3):
            w_relay(j, k).wait_recv()
        w_mate(j, 2).start()

    neg_start(0)
    w_send(0)
    w_send(1)
    neg_wait(0)
    neg_start(1)
    make_table(relation_ref, head_ref, tail_ref, table_ref, pos_ref, spots, here)
    at = 0
    for stage, to in ((1, 3), (2, 6), (3, 9), (4, 12), (5, 16)):
        send_steps(0, at, to)
        at = to
        neg_wait(stage)
        neg_start(stage + 1)
        if stage == 3:
            w_pass(0)
            w_pass(1)
    w_forward(0)
    w_forward(1)
    for j in (2, 3):
        w_copies[j].wait()
        w16[j, 0] = w32[j].astype(BF)
        w_send(j)
    send_steps(1, 0, 4)
    neg_wait(6)

    nt = (((1,), (1,)), ((), ()))
    tn = (((0,), (0,)), ((), ()))

    def back_copy(j, n, sign):
        return remote(out_back.at[j % 2, n], in_back.at[j, n], back_ss.at[j, n], back_rs.at[j, n], peer(j, n % 8, sign, here))

    def loss_copy(odd, d, sign):
        return remote(out_loss.at[odd, d // 4], in_loss.at[odd, d], loss_ss.at[odd, d], loss_rs.at[odd, d], peer(odd, d, sign, here))

    def score(j, i, c):
        k = (i + j // 2 * 2) % 4
        first = k * 8
        for d in range(1, 8):
            rows_copy(j, first + d, -1).wait_recv()
        slots = pl.ds(first, 8)
        h = in_rows[j, slots, 0:32, :].reshape(256, WIDTH)
        t = in_rows[j, slots, 32:64, :].reshape(256, WIDTH).astype(F32)
        w = w16.at[j, k]
        q = jnp.dot(h, w[...], preferred_element_type=F32).astype(BF)
        pos = jnp.sum(q.astype(F32) * t, axis=1, keepdims=True)
        s = lax.dot_general(q, neg[...], nt, preferred_element_type=F32)
        e = jnp.exp(-jnp.abs(s))
        soft = jnp.maximum(s, 0.0) + jnp.log1p(e)
        inv = 1.0 / (1.0 + e)
        coef = (jnp.where(s >= 0.0, inv, e * inv) * (1.0 / NEG)).astype(BF)
        g = jnp.dot(coef, neg[...], preferred_element_type=F32)
        ep = jnp.exp(-jnp.abs(pos))
        loss = jnp.maximum(-pos, 0.0) + jnp.log1p(ep) + jnp.sum(soft, axis=1, keepdims=True) * (1.0 / NEG)
        g = (g - jnp.where(pos <= 0.0, 1.0, ep) / (1.0 + ep) * t).astype(BF)
        back = lax.dot_general(g, w[...], nt, preferred_element_type=F32).astype(BF)
        if j >= 2:
            for d in range(1, 8):
                back_copy(j - 2, first + d, -1).wait_send()
        out_back[j % 2, slots] = back.reshape(8, CAP, WIDTH)
        for d in range(1, 8):
            back_copy(j, first + d, -1).start()
        in_back[j, first] = back[0:CAP]
        spot = lax.broadcasted_iota(I32, (256, 128), 1) == 0
        column = jnp.where(spot, loss, 0.0).astype(BF)
        row = lax.dot_general(jnp.ones((16, 128), BF), column, nt, preferred_element_type=F32).astype(BF)
        line = lax.broadcasted_iota(I32, (16, 128), 0) == (j // 2) * 4 + k
        for half in range(2):
            out_loss[j % 2, half] = jnp.where(line, row[:, half * 128 : half * 128 + 128], out_loss[j % 2, half])

        def outer(half):
            columns = pl.ds(pl.multiple_of(half * 256, 256), 256)
            return lax.dot_general(in_rows[j, slots, 0:32, columns].reshape(256, 256), g, tn, preferred_element_type=F32)

        if j >= 2:
            g1_copy(j - 2, k).wait_send()
        g1s[j % 2, k] = outer(1 - core).astype(BF)
        g1_copy(j, k).start()
        value = outer(core)

        @pl.when(k == 0)
        def _():
            own[j] = value

        @pl.when(k > 0)
        def _():
            if j >= 2:
                gy_copy(j - 2, k).wait_send()
            gys[j % 2, k] = value.astype(BF)

        @pl.when(i > 0)
        def _():
            g1_finish(j, (i - 1 + j // 2 * 2) % 4)

        return c

    def g1_copy(j, k):
        return remote(g1s.at[j % 2, k], g1r.at[j, k], g1_ss.at[j, k], g1_rs.at[j, k], mate)

    def gy_copy(j, k):
        device = device_at(core, x, (y + k * (1 - j % 2)) % 4, (z + k * (j % 2)) % 4)
        return remote(gys.at[j % 2, k], gyr.at[j, k], gy_ss.at[j, k], gy_rs.at[j, k], device)

    def g1_finish(j, k):
        g1_copy(j, k).wait_recv()

        @pl.when(k == 0)
        def _():
            own[j] = own[j] + g1r[j, 0].astype(F32)

        @pl.when(k > 0)
        def _():
            gys[j % 2, k] = (gys[j % 2, k].astype(F32) + g1r[j, k].astype(F32)).astype(BF)
            gy_copy(j, k).start()

    def gy_finish(j):
        for k in (1, 2, 3):
            gy_copy(j, k).wait_recv()
        own[j] = own[j] + gyr[j, 1].astype(F32) + gyr[j, 2].astype(F32) + gyr[j, 3].astype(F32)
        g2s[j] = own[j].astype(BF)
        g2_copy(j).start()

    def g2_copy(j):
        return remote(g2s.at[j], g2r.at[j], grp_ss.at[1, j], grp_rs.at[1, j], across)

    def g4_copies(j):
        part = rel_ref.at[j, rows_of(core * 256, 256)]
        tile = acc_ref.at[j, pl.ds(core * 2, 2)]
        return (
            remote(part, part, grp_ss.at[4, j], grp_rs.at[4, j], mate),
            remote(tile, tile, grp_ss.at[5, j], grp_rs.at[5, j], mate),
        )

    def g2_finish(j):
        g2_copy(j).wait_recv()
        eye = lax.broadcasted_iota(I32, (128, 128), 0) == lax.broadcasted_iota(I32, (128, 128), 1)
        for part in range(2):
            here_rows = slice(part * 128, part * 128 + 128)
            total = g2s[j, here_rows, :].astype(F32) + g2r[j, here_rows, :].astype(F32)
            quarter = core * 2 + part
            before = accum_ref[j : j + 1, pl.ds(pl.multiple_of(quarter * 128, 128), 128)]
            before = jnp.sum(jnp.where(eye, before, 0.0), axis=1, keepdims=True)
            after = before + jnp.sum(total * total, axis=1, keepdims=True) * (1.0 / WIDTH)
            rows = rows_of(quarter * 128, 128)
            rel_ref[j, rows, :] = (w32[j, rows, :] - total / jnp.sqrt(after)).astype(BF)
            line = jnp.sum(jnp.where(eye, after, 0.0), axis=0, keepdims=True)
            acc_ref[j, quarter] = jnp.broadcast_to(line, (8, 128))
        for copy in g4_copies(j):
            copy.start()

    def collect_wait(j, low, high):
        for n in range(low, high):
            if n % 8 > 0:
                back_copy(j, n, 1).wait_recv()

    def grad_copy(i):
        rows = rows_of(i * 256, 256)
        return pltpu.make_async_copy(grad_ref.at[rows], grad_out.at[rows], grad_sem.at[i])

    def collect(j, low, high, first=0, last=8, final=False):
        def block(i, c):
            rows = pl.ds(pl.multiple_of(i * 256, 256), 256)
            slot = lax.broadcasted_iota(I32, (256, (high - low) * CAP), 1) + (j * SLOTS + low) * CAP
            pick = jnp.where(pos_ref[rows, :] == slot, 1.0, 0.0).astype(BF)
            stack = in_back[j, low:high].reshape((high - low) * CAP, WIDTH)
            part = jnp.dot(pick, stack, preferred_element_type=F32).astype(BF)
            if j == 0:
                grad_ref[rows, :] = part
            else:
                grad_ref[rows, :] = grad_ref[rows, :] + part
            if final:
                grad_copy(i).start()
            return c

        lax.fori_loop(first, last, block, 0)

    def send_losses():
        for odd in range(2):
            in_loss[odd, 0] = out_loss[odd, 0]
            for d in range(1, 8):
                loss_copy(odd, d, -1).start()

    def collect_losses():
        group = lax.broadcasted_iota(I32, (16, 128), 1) // CAP
        tiles = []
        for odd in range(2):
            for half in range(2):
                value = jnp.zeros((16, 128), F32)
                for m in range(4):
                    if half + m > 0:
                        loss_copy(odd, half * 4 + m, 1).wait_recv()
                    value = jnp.where(group == m, in_loss[odd, half * 4 + m].astype(F32), value)
                tiles.append(value)
        stack = jnp.concatenate(tiles, axis=0).astype(BF)
        line = lax.broadcasted_iota(I32, (64, 128), 0)
        full = lax.broadcasted_iota(I32, (128, 128), 0)
        for i in range(ROWS // 128):
            spot = spots[i : i + 1, :]
            j = spot // 1024
            row = (j % 2) * 32 + (spot // 128 % 2) * 16 + (j // 2) * 4 + spot // 256 % 4
            pick = jnp.where(line == row, 1.0, 0.0).astype(BF)
            found = lax.dot_general(stack, pick, tn, preferred_element_type=F32)
            loss_ref[i : i + 1, :] = jnp.sum(jnp.where(full == spot % 128, found, 0.0), axis=0, keepdims=True)

    def g4_finish(j):
        for copy in g4_copies(j):
            copy.wait_recv()
        for q in range(4):
            acc_out[j : j + 1, q * 128 : q * 128 + 128] = acc_ref[j, q, 0:1]
        w32[j] = rel_ref[j].astype(F32)
        pltpu.make_async_copy(w32.at[j], new_ref.at[j], new_sem.at[j]).start()

    for j in range(CHUNKS):
        for k in (1, 2, 3):
            w_mate(j, k).wait_recv()
        if j == 0:

            def mixed(i, c):
                score(0, i, c)

                @pl.when(i < 3)
                def _():
                    send_steps(1, i * 4 + 4, i * 4 + 8)

                return c

            lax.fori_loop(0, 4, mixed, 0)
            w_pass(2)
            w_pass(3)
        else:
            lax.fori_loop(0, 4, lambda i, c, j=j: score(j, i, c), 0)
        if j == 1:
            w_forward(2)
            w_forward(3)
        if j == CHUNKS - 1:
            send_losses()
        g1_finish(j, (3 + j // 2 * 2) % 4)
        if j >= 1:
            gy_finish(j - 1)
        if j >= 2:
            g2_finish(j - 2)
        if j >= 3:
            g4_finish(j - 3)
        if j >= 1:
            collect_wait(j - 1, 0, SLOTS)
            collect(j - 1, 0, SLOTS)
    g2_finish(2)
    g4_finish(1)
    collect_wait(3, 16, 32)
    collect(3, 16, 32)
    gy_finish(3)
    collect_wait(3, 0, 16)
    collect(3, 0, 16, 0, 4, final=True)
    g2_finish(3)
    g4_finish(2)
    collect(3, 0, 16, 4, 8, final=True)
    collect_losses()
    g4_finish(3)

    for j in range(CHUNKS):
        for k in (1, 2, 3):
            w_mate(j, k).wait_send()
        for k in (1, 3):
            w_ring(j, k).wait_send()
            w_relay(j, k).wait_send()
        if j >= 2:
            for n in range(SLOTS):
                if n % 8 > 0:
                    rows_copy(j, n, 1).wait_send()
                    back_copy(j, n, -1).wait_send()
            for k in range(4):
                g1_copy(j, k).wait_send()
            for k in (1, 2, 3):
                gy_copy(j, k).wait_send()
        for copy in (g2_copy(j), *g4_copies(j)):
            copy.wait_send()
        pltpu.make_async_copy(w32.at[j], new_ref.at[j], new_sem.at[j]).wait()
    for odd in range(2):
        for d in range(1, 8):
            loss_copy(odd, d, -1).wait_send()
    for i in range(8):
        grad_copy(i).wait()


def per_device(head_ids, relations, tail_ids, neg_owner, entities, rel_weight, rel_accum):
    vmem, anywhere = pl.BlockSpec(memory_space=pltpu.VMEM), pl.BlockSpec(memory_space=pl.ANY)
    tiles = (ROWS // 128, 128)
    dma = pltpu.SemaphoreType.DMA
    scratch = [
        pltpu.VMEM((ROWS, WIDTH), BF),
        pltpu.VMEM((64, 128), F32),
        pltpu.VMEM((ROWS, 1), I32),
        pltpu.VMEM((16, 128), I32),
        pltpu.VMEM((CHUNKS, WIDTH, WIDTH), BF),
        pltpu.VMEM((CHUNKS, 4, 8, 128), F32),
        pltpu.VMEM((2, SLOTS, 64, WIDTH), BF),
        pltpu.VMEM((CHUNKS, SLOTS, 64, WIDTH), BF),
        pltpu.VMEM((2, SLOTS, CAP, WIDTH), BF),
        pltpu.VMEM((CHUNKS, SLOTS, CAP, WIDTH), BF),
        pltpu.VMEM((2, 2, 16, 128), BF),
        pltpu.VMEM((2, 8, 16, 128), BF),
        pltpu.VMEM((CHUNKS, WIDTH, WIDTH), F32),
        pltpu.VMEM((CHUNKS, 4, WIDTH, WIDTH), BF),
        pltpu.VMEM((CHUNKS, 256, WIDTH), F32),
        pltpu.VMEM((2, 4, 256, WIDTH), BF),
        pltpu.VMEM((CHUNKS, 4, 256, WIDTH), BF),
        pltpu.VMEM((2, 4, 256, WIDTH), BF),
        pltpu.VMEM((CHUNKS, 4, 256, WIDTH), BF),
        pltpu.VMEM((CHUNKS, 256, WIDTH), BF),
        pltpu.VMEM((CHUNKS, 256, WIDTH), BF),
        pltpu.VMEM((NEG, WIDTH), BF),
        pltpu.VMEM((512, WIDTH), BF),
        pltpu.VMEM((512, WIDTH), BF),
        pltpu.VMEM((512, WIDTH), BF),
        pltpu.VMEM((3, 128, WIDTH), BF),
        pltpu.VMEM((128, WIDTH), BF),
        pltpu.VMEM((3, 32, WIDTH), BF),
        pltpu.VMEM((32, WIDTH), BF),
        pltpu.VMEM((3, 32, WIDTH), BF),
        pltpu.VMEM((32, WIDTH), BF),
        dma((CHUNKS,)),
        dma((CHUNKS,)),
        dma((8,)),
        *[dma((CHUNKS, SLOTS))] * 4,
        *[dma((2, 8))] * 2,
        *[dma((CHUNKS, 4))] * 8,
        *[dma((7, 3))] * 2,
        *[dma((6, CHUNKS))] * 2,
    ]
    head_grad, losses, new_rel, new_accum = pl.pallas_call(
        main_kernel,
        out_shape=(
            jax.ShapeDtypeStruct((ROWS, WIDTH), BF),
            jax.ShapeDtypeStruct((16, 128), F32),
            jax.ShapeDtypeStruct((CHUNKS, WIDTH, WIDTH), F32),
            jax.ShapeDtypeStruct((CHUNKS, WIDTH), F32),
        ),
        in_specs=[pl.BlockSpec(memory_space=pltpu.SMEM), *[vmem] * 5, anywhere],
        out_specs=(anywhere, vmem, anywhere, vmem),
        scratch_shapes=scratch,
        compiler_params=pltpu.CompilerParams(collective_id=0, has_side_effects=True, vmem_limit_bytes=VMEM_BYTES),
        name="rescal",
    )(neg_owner, entities, relations.reshape(tiles), head_ids.reshape(tiles), tail_ids.reshape(tiles), rel_accum, rel_weight)
    return losses.reshape(ROWS).astype(BF), head_grad, new_rel, new_accum


def solution(mesh):
    placed = (
        P(("grp", "rel")),
        P(("grp", "rel"), None),
        P(("grp", "rel")),
        P(),
        P(("grp", "rel"), None),
        P("rel", None, None),
        P("rel", None),
    )
    return jax.shard_map(
        per_device,
        mesh=mesh,
        in_specs=placed,
        out_specs=(
            P(("grp", "rel")),
            P(("grp", "rel"), None),
            P("rel", None, None),
            P("rel", None),
        ),
        check_vma=False,
    )
```

```python
import jax
import jax.numpy as jnp
from jax import lax
from jax.experimental import pallas as pl
from jax.experimental.pallas import tpu as pltpu
from jax.sharding import PartitionSpec as P

MESH = pl.DeviceIdType.MESH
BF, F32, I32 = jnp.bfloat16, jnp.float32, jnp.int32
ROWS, WIDTH, NEG = 2048, 512, 1024
CHUNKS, SLOTS, CAP = 4, 32, 32
VMEM_BYTES = 61 * 2**20


def place():
    grp, rel = lax.axis_index("grp"), lax.axis_index("rel")
    x_hi, core = grp // 2, grp % 2
    x_lo, y, z = rel // 16, (rel // 4) % 4, rel % 4
    return x_hi, core, x_hi * 2 + x_lo, x_lo, y, z


def device_at(core, x, y, z):
    return ((x // 2) * 2 + core, (x % 2) * 16 + y * 4 + z)


def peer(j, d, sign, here):
    x_hi, core, x, x_lo, y, z = here
    dx, dm, odd = d % 2, d // 2, j % 2
    x = (x + dx * (1 + 2 * (x % 2) + 2 * (dm % 2))) % 4
    return device_at(core, x, (y + sign * dm * odd + 4) % 4, (z + sign * dm * (1 - odd) + 4) % 4)


def make_table(rel_ref, head_ref, tail_ref, table, pos, spots, here):
    x_hi, core, x, x_lo, y, z = here
    line = lax.broadcasted_iota(I32, (128, 128), 0)
    lane = lax.broadcasted_iota(I32, (128, 128), 1)
    earlier = jnp.where(line < lane, 1.0, 0.0).astype(BF)
    seen = jnp.zeros((128, 1), F32)
    total = jnp.zeros((128, 128), F32)
    for i in range(ROWS // 128):
        rel, head, tail = rel_ref[i : i + 1, :], head_ref[i : i + 1, :] + 1, tail_ref[i : i + 1, :] + 1
        hot = jnp.where(line == rel, 1.0, 0.0)
        before = jnp.dot(hot.astype(BF), earlier, preferred_element_type=F32) + seen
        rank = jnp.sum(hot * before, axis=0, keepdims=True).astype(I32)
        digit = jnp.where(line < 64, jnp.where(line < 32, head // 32, head % 32), jnp.where(line < 96, tail // 32, tail % 32))
        marks = jnp.where(line % 32 == rank, digit, 0).astype(F32).astype(BF)
        total = total + lax.dot_general(marks, hot.astype(BF), (((1,), (1,)), ((), ())), preferred_element_type=F32)
        seen = seen + jnp.sum(hot, axis=1, keepdims=True)
        owner = rel // 4
        dy, dz = (owner // 4 % 4 + 4 - y) % 4, (owner % 4 + 4 - z) % 4
        dx, odd = (owner // 16 + 2 - x_lo) % 2, rel % 2
        dm, dk = dy * odd + dz * (1 - odd), dz * odd + dy * (1 - odd)
        spot = (rel % 4) * (SLOTS * CAP) + (dk * 8 + dm * 2 + dx) * CAP + rank
        spots[i : i + 1, :] = spot
        pos[i * 128 : i * 128 + 128, :] = jnp.sum(jnp.where(line == lane, spot, 0), axis=1, keepdims=True)
    table[0:32, :] = total[0:32] * 32.0 + total[32:64] - 1.0
    table[32:64, :] = total[64:96] * 32.0 + total[96:128] - 1.0


def main_kernel(
    owner_ref, ent_ref, relation_ref, head_ref, tail_ref, accum_ref, weight_ref,
    grad_out, loss_ref, new_ref, acc_out,
    grad_ref,    table_ref, pos_ref, spots, rel_ref, acc_ref,
    out_rows, in_rows, out_back, in_back, out_loss, in_loss, w32, w16,
    own, g1s, g1r, gys, gyr, g2s, g2r,
    neg, n0s, n0r, n1, n1r, n2, n2r, n3, n3r, n4,
    w_sem, new_sem, grad_sem, rows_ss, rows_rs, back_ss, back_rs, loss_ss, loss_rs,
    wr_ss, wr_rs, wm_ss, wm_rs, g1_ss, g1_rs, gy_ss, gy_rs, neg_ss, neg_rs, grp_ss, grp_rs,
):
    here = place()
    x_hi, core, x, x_lo, y, z = here
    me = lax.axis_index("grp") * 32 + lax.axis_index("rel")
    mate = device_at(1 - core, x, y, z)
    across = device_at(core, (x + 2) % 4, y, z)
    beside = device_at(core, (x + 3 + 2 * (x % 2)) % 4, y, z)

    def remote(src, dst, ss, rs, device):
        return pltpu.make_async_remote_copy(src_ref=src, dst_ref=dst, send_sem=ss, recv_sem=rs, device_id=device, device_id_type=MESH)

    w_copies = [pltpu.make_async_copy(weight_ref.at[j], w32.at[j], w_sem.at[j]) for j in range(CHUNKS)]
    for copy in w_copies:
        copy.start()

    barrier = pltpu.get_barrier_semaphore()

    def greet(device):
        pl.semaphore_signal(barrier, inc=1, device_id=device, device_id_type=MESH)

    for d in range(1, 8):
        greet(peer(0, d, 1, here))
    for d in range(2, 8):
        greet(peer(1, d, 1, here))
    for device in (mate, across, beside):
        greet(device)
    out_loss[...] = jnp.zeros_like(out_loss)
    for j in range(2):
        w_copies[j].wait()
        w16[j, 0] = w32[j].astype(BF)
    pl.semaphore_wait(barrier, 16)

    mine = (owner_ref[0] == me).astype(F32).astype(BF)

    def ring(axis, d):
        if axis == 0:
            return device_at(core, (x + d) % 4, y, z), (x + d) % 4
        if axis == 1:
            return device_at(core, x, (y + d) % 4, z), (y + d) % 4
        return device_at(core, x, y, (z + d) % 4), (z + d) % 4

    def rows_of(start, size):
        return pl.ds(pl.multiple_of(start, size), size)

    block32 = core * 512 + x * 128 + y * 32

    def neg_copies(stage):
        if stage == 0:
            return [remote(n0s, n0r, neg_ss.at[0, 0], neg_rs.at[0, 0], mate)]
        if stage == 6:
            part = neg.at[rows_of(core * 512, 512)]
            return [remote(part, part, neg_ss.at[6, 0], neg_rs.at[6, 0], mate)]
        copies = []
        for d in (1, 2, 3):
            sems = neg_ss.at[stage, d - 1], neg_rs.at[stage, d - 1]
            device, there = ring({1: 0, 2: 1, 3: 2, 4: 1, 5: 0}[stage], d)
            if stage == 1:
                copies.append(remote(n1.at[rows_of(there * 128, 128)], n1r.at[d - 1], *sems, device))
            elif stage == 2:
                copies.append(remote(n2.at[rows_of(there * 32, 32)], n2r.at[d - 1], *sems, device))
            elif stage == 3:
                copies.append(remote(n3, n3r.at[d - 1], *sems, device))
            elif stage == 4:
                copies.append(remote(n4, neg.at[rows_of(block32, 32)], *sems, device))
            else:
                part = neg.at[rows_of(core * 512 + x * 128, 128)]
                copies.append(remote(part, part, *sems, device))
        return copies

    def neg_start(stage):
        if stage == 0:
            n0s[...] = ent_ref[rows_of((1 - core) * 512, 512), :] * mine
        elif stage == 1:
            n1[...] = ent_ref[rows_of(core * 512, 512), :] * mine + n0r[...]
        elif stage == 2:
            n2[...] = n1[rows_of(x * 128, 128), :] + n1r[0] + n1r[1] + n1r[2]
        elif stage == 3:
            n3[...] = n2[rows_of(y * 32, 32), :] + n2r[0] + n2r[1] + n2r[2]
        elif stage == 4:
            total = n3[...] + n3r[0] + n3r[1] + n3r[2]
            n4[...] = total
            neg[rows_of(block32, 32), :] = total
        for copy in neg_copies(stage):
            copy.start()

    def neg_wait(stage):
        for copy in neg_copies(stage):
            copy.wait()

    def rows_copy(j, n, sign):
        return remote(out_rows.at[j % 2, n], in_rows.at[j, n], rows_ss.at[j, n], rows_rs.at[j, n], peer(j, n % 8, sign, here))

    lane128 = lax.broadcasted_iota(I32, (64, 128), 1)
    lane1024 = lax.broadcasted_iota(I32, (64, NEG), 1).astype(F32)

    def send_rows(pair, i):
        j, odd = 2 * pair + i % 2, i % 2
        k = (i // 4 + 2 * pair) % 4
        first = k * 8 + (i // 2 % 2) * 4
        hots = []
        for m in range(4):
            d = (first + m) % 8
            dm = d // 2
            oy = (y + dm * odd + k * (1 - odd)) % 4
            oz = (z + dm * (1 - odd) + k * odd) % 4
            owner = ((x_lo + d) % 2) * 16 + oy * 4 + oz
            ids = jnp.sum(jnp.where(lane128 == owner * 4 + j, table_ref[...], 0.0), axis=1, keepdims=True)
            hots.append(jnp.where(lane1024 == ids, 1.0, 0.0).astype(BF))
        rows = jnp.dot(jnp.concatenate(hots, axis=0), ent_ref[...], preferred_element_type=F32).astype(BF)
        local = i // 2 % 2 == 0
        for m in range(4):
            if pair > 0:
                if m == 0:

                    @pl.when(jnp.logical_not(local))
                    def _():
                        rows_copy(j - 2, first, 1).wait_send()

                else:
                    rows_copy(j - 2, first + m, 1).wait_send()
        out_rows[j % 2, pl.ds(first, 4)] = rows.reshape(4, 64, WIDTH)
        for m in range(4):
            if m == 0:

                @pl.when(local)
                def _():
                    in_rows[j, first] = rows[0:64]

                @pl.when(jnp.logical_not(local))
                def _():
                    rows_copy(j, first, 1).start()

            else:
                rows_copy(j, first + m, 1).start()

    def send_steps(pair, first, last):
        def body(i, c):
            send_rows(pair, i)
            return c

        lax.fori_loop(first, last, body, 0)

    my_half = rows_of(core * 256, 256)

    def w_ring(j, k):
        device = device_at(core, x, (y + (4 - k) * (1 - j % 2)) % 4, (z + (4 - k) * (j % 2)) % 4)
        return remote(w16.at[j, 0, my_half], w16.at[j, k, my_half], wr_ss.at[j, k], wr_rs.at[j, k], device)

    def w_mate(j, k):
        part = w16.at[j, k, my_half]
        return remote(part, part, wm_ss.at[j, k], wm_rs.at[j, k], mate)

    def w_relay(j, k):
        part = rows_of(core * 256 + (k // 2) * 128, 128)
        device = device_at(core, x, (y + (4 - k) * (1 - j % 2)) % 4, (z + (4 - k) * (j % 2)) % 4)
        return remote(w16.at[j, k, part], w16.at[j, 2, part], wr_ss.at[j, k - 1], wr_rs.at[j, k - 1], device)

    def w_send(j):
        for k in (1, 3):
            w_ring(j, k).start()

    def w_pass(j):
        for k in (1, 3):
            w_ring(j, k).wait_recv()
            w_relay(j, k).start()
            w_mate(j, k).start()

    def w_forward(j):
        for k in (1, 3):
            w_relay(j, k).wait_recv()
        w_mate(j, 2).start()

    neg_start(0)
    w_send(0)
    w_send(1)
    neg_wait(0)
    neg_start(1)
    make_table(relation_ref, head_ref, tail_ref, table_ref, pos_ref, spots, here)
    at = 0
    for stage, to in ((1, 3), (2, 6), (3, 9), (4, 12), (5, 16)):
        send_steps(0, at, to)
        at = to
        neg_wait(stage)
        neg_start(stage + 1)
        if stage == 3:
            w_pass(0)
            w_pass(1)
    w_forward(0)
    w_forward(1)
    for j in (2, 3):
        w_copies[j].wait()
        w16[j, 0] = w32[j].astype(BF)
        w_send(j)
    send_steps(1, 0, 4)
    neg_wait(6)

    nt = (((1,), (1,)), ((), ()))
    tn = (((0,), (0,)), ((), ()))

    def back_copy(j, n, sign):
        return remote(out_back.at[j % 2, n], in_back.at[j, n], back_ss.at[j, n], back_rs.at[j, n], peer(j, n % 8, sign, here))

    def loss_copy(odd, d, sign):
        return remote(out_loss.at[odd, d // 4], in_loss.at[odd, d], loss_ss.at[odd, d], loss_rs.at[odd, d], peer(odd, d, sign, here))

    def score(j, i, c):
        k = (i + j // 2 * 2) % 4
        first = k * 8
        for d in range(1, 8):
            rows_copy(j, first + d, -1).wait_recv()
        slots = pl.ds(first, 8)
        h = in_rows[j, slots, 0:32, :].reshape(256, WIDTH)
        t = in_rows[j, slots, 32:64, :].reshape(256, WIDTH).astype(F32)
        w = w16.at[j, k]
        q = jnp.dot(h, w[...], preferred_element_type=F32).astype(BF)
        pos = jnp.sum(q.astype(F32) * t, axis=1, keepdims=True)
        s = lax.dot_general(q, neg[...], nt, preferred_element_type=F32)
        e = jnp.exp(-jnp.abs(s))
        soft = jnp.maximum(s, 0.0) + jnp.log1p(e)
        inv = 1.0 / (1.0 + e)
        coef = (jnp.where(s >= 0.0, inv, e * inv) * (1.0 / NEG)).astype(BF)
        g = jnp.dot(coef, neg[...], preferred_element_type=F32)
        ep = jnp.exp(-jnp.abs(pos))
        loss = jnp.maximum(-pos, 0.0) + jnp.log1p(ep) + jnp.sum(soft, axis=1, keepdims=True) * (1.0 / NEG)
        g = (g - jnp.where(pos <= 0.0, 1.0, ep) / (1.0 + ep) * t).astype(BF)
        back = lax.dot_general(g, w[...], nt, preferred_element_type=F32).astype(BF)
        if j >= 2:
            for d in range(1, 8):
                back_copy(j - 2, first + d, -1).wait_send()
        out_back[j % 2, slots] = back.reshape(8, CAP, WIDTH)
        for d in range(1, 8):
            back_copy(j, first + d, -1).start()
        in_back[j, first] = back[0:CAP]
        spot = lax.broadcasted_iota(I32, (256, 128), 1) == 0
        column = jnp.where(spot, loss, 0.0).astype(BF)
        row = lax.dot_general(jnp.ones((16, 128), BF), column, nt, preferred_element_type=F32).astype(BF)
        line = lax.broadcasted_iota(I32, (16, 128), 0) == (j // 2) * 4 + k
        for half in range(2):
            out_loss[j % 2, half] = jnp.where(line, row[:, half * 128 : half * 128 + 128], out_loss[j % 2, half])

        def outer(half):
            columns = pl.ds(pl.multiple_of(half * 256, 256), 256)
            return lax.dot_general(in_rows[j, slots, 0:32, columns].reshape(256, 256), g, tn, preferred_element_type=F32)

        if j >= 2:
            g1_copy(j - 2, k).wait_send()
        g1s[j % 2, k] = outer(1 - core).astype(BF)
        g1_copy(j, k).start()
        value = outer(core)

        @pl.when(k == 0)
        def _():
            own[j] = value

        @pl.when(k > 0)
        def _():
            if j >= 2:

                @pl.when(k == 2)
                def _():
                    gz_copy(j - 2, 1).wait_send()
                    gz_copy(j - 2, 3).wait_send()

                @pl.when(k != 2)
                def _():
                    gy_copy(j - 2, k).wait_send()

            gys[j % 2, k] = value.astype(BF)

        @pl.when(i > 0)
        def _():
            g1_finish(j, (i - 1 + j // 2 * 2) % 4)

        return c

    def g1_copy(j, k):
        return remote(g1s.at[j % 2, k], g1r.at[j, k], g1_ss.at[j, k], g1_rs.at[j, k], mate)

    def gy_copy(j, k):
        device = device_at(core, x, (y + k * (1 - j % 2)) % 4, (z + k * (j % 2)) % 4)
        return remote(gys.at[j % 2, k], gyr.at[j, k], gy_ss.at[j, k], gy_rs.at[j, k], device)

    def gz_copy(j, k):
        device = device_at(core, x, (y + k * (1 - j % 2)) % 4, (z + k * (j % 2)) % 4)
        half = pl.ds((k // 2) * 128, 128)
        return remote(gys.at[j % 2, 2, half], gyr.at[j, k - 1, pl.ds(0, 128)], gy_ss.at[j, k - 1], gy_rs.at[j, k - 1], device)

    def gz_finish(j):
        for k in (1, 3):
            gz_copy(j, k).wait_recv()
            half = slice((k // 2) * 128, (k // 2) * 128 + 128)
            gys[j % 2, k, half, :] = (gys[j % 2, k, half, :].astype(F32) + gyr[j, k - 1, 0:128, :].astype(F32)).astype(BF)
            gy_copy(j, k).start()

    def g1_finish(j, k):
        g1_copy(j, k).wait_recv()

        @pl.when(k == 0)
        def _():
            own[j] = own[j] + g1r[j, 0].astype(F32)

        @pl.when(k > 0)
        def _():
            gys[j % 2, k] = (gys[j % 2, k].astype(F32) + g1r[j, k].astype(F32)).astype(BF)

        @pl.when(k == 2)
        def _():
            gz_copy(j, 1).start()
            gz_copy(j, 3).start()

    def gy_finish(j):
        for k in (1, 3):
            gy_copy(j, k).wait_recv()
        own[j] = own[j] + gyr[j, 1].astype(F32) + gyr[j, 3].astype(F32)
        g2s[j] = own[j].astype(BF)
        g2_copy(j).start()

    def g2_copy(j):
        return remote(g2s.at[j], g2r.at[j], grp_ss.at[1, j], grp_rs.at[1, j], across)

    def g4_copies(j):
        part = rel_ref.at[j, rows_of(core * 256, 256)]
        tile = acc_ref.at[j, pl.ds(core * 2, 2)]
        return (
            remote(part, part, grp_ss.at[4, j], grp_rs.at[4, j], mate),
            remote(tile, tile, grp_ss.at[5, j], grp_rs.at[5, j], mate),
        )

    def g2_finish(j):
        g2_copy(j).wait_recv()
        eye = lax.broadcasted_iota(I32, (128, 128), 0) == lax.broadcasted_iota(I32, (128, 128), 1)
        for part in range(2):
            here_rows = slice(part * 128, part * 128 + 128)
            total = g2s[j, here_rows, :].astype(F32) + g2r[j, here_rows, :].astype(F32)
            quarter = core * 2 + part
            before = accum_ref[j : j + 1, pl.ds(pl.multiple_of(quarter * 128, 128), 128)]
            before = jnp.sum(jnp.where(eye, before, 0.0), axis=1, keepdims=True)
            after = before + jnp.sum(total * total, axis=1, keepdims=True) * (1.0 / WIDTH)
            rows = rows_of(quarter * 128, 128)
            rel_ref[j, rows, :] = (w32[j, rows, :] - total / jnp.sqrt(after)).astype(BF)
            line = jnp.sum(jnp.where(eye, after, 0.0), axis=0, keepdims=True)
            acc_ref[j, quarter] = jnp.broadcast_to(line, (8, 128))
        for copy in g4_copies(j):
            copy.start()

    def collect_wait(j, low, high):
        for n in range(low, high):
            if n % 8 > 0:
                back_copy(j, n, 1).wait_recv()

    def grad_copy(i):
        rows = rows_of(i * 256, 256)
        return pltpu.make_async_copy(grad_ref.at[rows], grad_out.at[rows], grad_sem.at[i])

    def collect(j, low, high, first=0, last=8, final=False):
        def block(i, c):
            rows = pl.ds(pl.multiple_of(i * 256, 256), 256)
            slot = lax.broadcasted_iota(I32, (256, (high - low) * CAP), 1) + (j * SLOTS + low) * CAP
            pick = jnp.where(pos_ref[rows, :] == slot, 1.0, 0.0).astype(BF)
            stack = in_back[j, low:high].reshape((high - low) * CAP, WIDTH)
            part = jnp.dot(pick, stack, preferred_element_type=F32).astype(BF)
            if j == 0:
                grad_ref[rows, :] = part
            else:
                grad_ref[rows, :] = grad_ref[rows, :] + part
            if final:
                grad_copy(i).start()
            return c

        lax.fori_loop(first, last, block, 0)

    def send_losses():
        for odd in range(2):
            in_loss[odd, 0] = out_loss[odd, 0]
            for d in range(1, 8):
                loss_copy(odd, d, -1).start()

    def collect_losses():
        group = lax.broadcasted_iota(I32, (16, 128), 1) // CAP
        tiles = []
        for odd in range(2):
            for half in range(2):
                value = jnp.zeros((16, 128), F32)
                for m in range(4):
                    if half + m > 0:
                        loss_copy(odd, half * 4 + m, 1).wait_recv()
                    value = jnp.where(group == m, in_loss[odd, half * 4 + m].astype(F32), value)
                tiles.append(value)
        stack = jnp.concatenate(tiles, axis=0).astype(BF)
        line = lax.broadcasted_iota(I32, (64, 128), 0)
        full = lax.broadcasted_iota(I32, (128, 128), 0)
        for i in range(ROWS // 128):
            spot = spots[i : i + 1, :]
            j = spot // 1024
            row = (j % 2) * 32 + (spot // 128 % 2) * 16 + (j // 2) * 4 + spot // 256 % 4
            pick = jnp.where(line == row, 1.0, 0.0).astype(BF)
            found = lax.dot_general(stack, pick, tn, preferred_element_type=F32)
            loss_ref[i : i + 1, :] = jnp.sum(jnp.where(full == spot % 128, found, 0.0), axis=0, keepdims=True)

    def g4_finish(j):
        for copy in g4_copies(j):
            copy.wait_recv()
        for q in range(4):
            acc_out[j : j + 1, q * 128 : q * 128 + 128] = acc_ref[j, q, 0:1]
        w32[j] = rel_ref[j].astype(F32)
        pltpu.make_async_copy(w32.at[j], new_ref.at[j], new_sem.at[j]).start()

    for j in range(CHUNKS):
        for k in (1, 2, 3):
            w_mate(j, k).wait_recv()
        if j == 0:

            def mixed(i, c):
                score(0, i, c)

                @pl.when(i < 3)
                def _():
                    send_steps(1, i * 4 + 4, i * 4 + 8)

                return c

            lax.fori_loop(0, 4, mixed, 0)
            w_pass(2)
            w_pass(3)
        else:
            lax.fori_loop(0, 4, lambda i, c, j=j: score(j, i, c), 0)
        if j == 1:
            w_forward(2)
            w_forward(3)
        if j == CHUNKS - 1:
            send_losses()
        g1_finish(j, (3 + j // 2 * 2) % 4)
        if j == CHUNKS - 1:
            gz_finish(j)
        if j >= 1:
            gy_finish(j - 1)
        if j >= 2:
            g2_finish(j - 2)
        if j >= 3:
            g4_finish(j - 3)
        if j >= 1:
            collect_wait(j - 1, 0, SLOTS)
            collect(j - 1, 0, SLOTS)
        if j < CHUNKS - 1:
            gz_finish(j)
    g2_finish(2)
    g4_finish(1)
    collect_wait(3, 16, 32)
    collect(3, 16, 32)
    gy_finish(3)
    collect_wait(3, 0, 16)
    collect(3, 0, 16, 0, 4, final=True)
    g2_finish(3)
    g4_finish(2)
    collect(3, 0, 16, 4, 8, final=True)
    collect_losses()
    g4_finish(3)

    for j in range(CHUNKS):
        for k in (1, 2, 3):
            w_mate(j, k).wait_send()
        for k in (1, 3):
            w_ring(j, k).wait_send()
            w_relay(j, k).wait_send()
        if j >= 2:
            for n in range(SLOTS):
                if n % 8 > 0:
                    rows_copy(j, n, 1).wait_send()
                    back_copy(j, n, -1).wait_send()
            for k in range(4):
                g1_copy(j, k).wait_send()
            for k in (1, 3):
                gy_copy(j, k).wait_send()
                gz_copy(j, k).wait_send()
        for copy in (g2_copy(j), *g4_copies(j)):
            copy.wait_send()
        pltpu.make_async_copy(w32.at[j], new_ref.at[j], new_sem.at[j]).wait()
    for odd in range(2):
        for d in range(1, 8):
            loss_copy(odd, d, -1).wait_send()
    for i in range(8):
        grad_copy(i).wait()


def per_device(head_ids, relations, tail_ids, neg_owner, entities, rel_weight, rel_accum):
    vmem, anywhere = pl.BlockSpec(memory_space=pltpu.VMEM), pl.BlockSpec(memory_space=pl.ANY)
    tiles = (ROWS // 128, 128)
    dma = pltpu.SemaphoreType.DMA
    scratch = [
        pltpu.VMEM((ROWS, WIDTH), BF),
        pltpu.VMEM((64, 128), F32),
        pltpu.VMEM((ROWS, 1), I32),
        pltpu.VMEM((16, 128), I32),
        pltpu.VMEM((CHUNKS, WIDTH, WIDTH), BF),
        pltpu.VMEM((CHUNKS, 4, 8, 128), F32),
        pltpu.VMEM((2, SLOTS, 64, WIDTH), BF),
        pltpu.VMEM((CHUNKS, SLOTS, 64, WIDTH), BF),
        pltpu.VMEM((2, SLOTS, CAP, WIDTH), BF),
        pltpu.VMEM((CHUNKS, SLOTS, CAP, WIDTH), BF),
        pltpu.VMEM((2, 2, 16, 128), BF),
        pltpu.VMEM((2, 8, 16, 128), BF),
        pltpu.VMEM((CHUNKS, WIDTH, WIDTH), F32),
        pltpu.VMEM((CHUNKS, 4, WIDTH, WIDTH), BF),
        pltpu.VMEM((CHUNKS, 256, WIDTH), F32),
        pltpu.VMEM((2, 4, 256, WIDTH), BF),
        pltpu.VMEM((CHUNKS, 4, 256, WIDTH), BF),
        pltpu.VMEM((2, 4, 256, WIDTH), BF),
        pltpu.VMEM((CHUNKS, 4, 256, WIDTH), BF),
        pltpu.VMEM((CHUNKS, 256, WIDTH), BF),
        pltpu.VMEM((CHUNKS, 256, WIDTH), BF),
        pltpu.VMEM((NEG, WIDTH), BF),
        pltpu.VMEM((512, WIDTH), BF),
        pltpu.VMEM((512, WIDTH), BF),
        pltpu.VMEM((512, WIDTH), BF),
        pltpu.VMEM((3, 128, WIDTH), BF),
        pltpu.VMEM((128, WIDTH), BF),
        pltpu.VMEM((3, 32, WIDTH), BF),
        pltpu.VMEM((32, WIDTH), BF),
        pltpu.VMEM((3, 32, WIDTH), BF),
        pltpu.VMEM((32, WIDTH), BF),
        dma((CHUNKS,)),
        dma((CHUNKS,)),
        dma((8,)),
        *[dma((CHUNKS, SLOTS))] * 4,
        *[dma((2, 8))] * 2,
        *[dma((CHUNKS, 4))] * 8,
        *[dma((7, 3))] * 2,
        *[dma((6, CHUNKS))] * 2,
    ]
    head_grad, losses, new_rel, new_accum = pl.pallas_call(
        main_kernel,
        out_shape=(
            jax.ShapeDtypeStruct((ROWS, WIDTH), BF),
            jax.ShapeDtypeStruct((16, 128), F32),
            jax.ShapeDtypeStruct((CHUNKS, WIDTH, WIDTH), F32),
            jax.ShapeDtypeStruct((CHUNKS, WIDTH), F32),
        ),
        in_specs=[pl.BlockSpec(memory_space=pltpu.SMEM), *[vmem] * 5, anywhere],
        out_specs=(anywhere, vmem, anywhere, vmem),
        scratch_shapes=scratch,
        compiler_params=pltpu.CompilerParams(collective_id=0, has_side_effects=True, vmem_limit_bytes=VMEM_BYTES),
        name="rescal",
    )(neg_owner, entities, relations.reshape(tiles), head_ids.reshape(tiles), tail_ids.reshape(tiles), rel_accum, rel_weight)
    return losses.reshape(ROWS).astype(BF), head_grad, new_rel, new_accum


def solution(mesh):
    placed = (
        P(("grp", "rel")),
        P(("grp", "rel"), None),
        P(("grp", "rel")),
        P(),
        P(("grp", "rel"), None),
        P("rel", None, None),
        P("rel", None),
    )
    return jax.shard_map(
        per_device,
        mesh=mesh,
        in_specs=placed,
        out_specs=(
            P(("grp", "rel")),
            P(("grp", "rel"), None),
            P("rel", None, None),
            P("rel", None),
        ),
        check_vma=False,
    )
```
